32 devices in a mesh: space: 8 (over z, x), sample: 4 (over y, core).
Axes of the slice: x: 2, y: 2, z: 4, core: 2. Of those that a mesh axis runs over, the one named last changes fastest.
Arguments:
- state_hat: float32 [20, 3, 64, 32, 128], P('sample', None, 'space'), may hold values from -2.4 to 2.4
- adjoint_hat: float32 [20, 3, 64, 32, 128], P('sample', None, 'space'), may hold values from -2.4 to 2.4
- objective_hat: float32 [20, 3, 64, 32, 128], P('sample', None, 'space'), may hold values from -6 to 6
- density: float32 [64, 32, 128], P('space'), may hold values from 0.05 to 1
- region: int32 [64, 32, 128], P('space'), may hold values from 0 to 3
Outputs:
- adjoint_residual: float32 [20, 3, 64, 32, 128], P('sample', None, 'space')
- density_gradient: float32 [64, 32, 128], P('space', 'sample')
The draws below stay inside these ranges and needn't reach their ends.
All inputs are finite; a program needn't handle non-finite values.
Results may differ from the reference program's by a relative error of at most 0.00026.
Values sent between devices are 32-bit elements; how exact they have to be, the bound alone decides.
No kernel may reach another device: no remote copies, remote signals or barrier semaphores. Data moves between devices by JAX's collectives and lax.ppermute only.
A program may use at most 128 MiB of HBM per device.

```python
import math
import jax
import jax.numpy as jnp
from jax import lax

NY = 32
NZ = 128
NCOEF = 20
NT = 40
NX = 64


def touch_ends(result, rng, smallest, largest):
    extent = result.shape
    spot = [jax.random.randint(jax.random.fold_in(rng, axis), (), 0, extent[axis]) for axis in range(len(extent))]
    result = result.at[tuple(spot)].set(smallest)
    longest = extent.index(max(extent))
    spot[longest] = (spot[longest] + 1) % extent[longest]
    return result.at[tuple(spot)].set(largest)


def block_scale(key, dims, pieces, low, largest):
    loudness = 1.0
    for dim, parts in pieces:
        heights = jax.random.uniform(jax.random.fold_in(jax.random.fold_in(key, 6), dim), (parts,), jnp.float32, low / len(pieces), largest / len(pieces))
        loudness = loudness * jnp.repeat(jnp.exp(heights), dims[dim] // parts).reshape((-1,) + (1,) * (len(dims) - 1 - dim))
    return loudness


def bell_draw(own_key, shape, width, reach, split=(), held_as=jnp.bfloat16):
    factor_of = block_scale(own_key, shape, split, -0.22, 0.18) if split else 1.0
    drawn = jax.random.normal(own_key, shape, jnp.float32) * width * factor_of
    return jnp.minimum(jnp.maximum(drawn, -reach), reach).astype(held_as)


def setup_inputs(seed: int = 0) -> dict:
    seeds = jax.random.split(jax.random.key(seed), 6)
    state_hat = bell_draw(seeds[0], (NCOEF, 3, NX, NY, NZ), 0.3, 2.4, ((0, 4), (2, 8)), jnp.float32)
    adjoint_hat = bell_draw(seeds[1], (NCOEF, 3, NX, NY, NZ), 0.3, 2.4, ((0, 4), (2, 8)), jnp.float32)
    objective_hat = bell_draw(seeds[2], (NCOEF, 3, NX, NY, NZ), 1.0, 6.0, ((0, 4), (2, 8)), jnp.float32)
    density = jnp.clip(0.05 + 0.95 * jax.random.uniform(seeds[3], (NX, NY, NZ), jnp.float32) ** block_scale(seeds[3], (NX, NY, NZ), ((0, 8),), -0.2, 0.2), 0.05, 1.0)
    region = touch_ends(jax.random.randint(seeds[4], (NX, NY, NZ), 0, 4), jax.random.fold_in(seeds[4], 1), 0, 3).astype(jnp.int32)
    return dict(state_hat=state_hat, adjoint_hat=adjoint_hat, objective_hat=objective_hat, density=density, region=region)


magnet_reluct = 0.95
iron_floor = 0.05
saturation = 1.0


def harmonic_table():
    sample_steps = jnp.arange(NT, dtype=jnp.int32).astype(jnp.float32)
    orders = (jnp.arange(NCOEF // 2, dtype=jnp.int32) + 1).astype(jnp.float32)
    angles = (2.0 * math.pi / NT) * sample_steps[:, None] * orders[None, :]
    return jnp.stack([jnp.cos(angles), jnp.sin(angles)], axis=2).reshape(NT, NCOEF)


def forward_diff(potential, along):
    length = potential.shape[along]
    widths = [(0, 0)] * potential.ndim
    widths[along] = (0, 1)
    padded = jnp.pad(potential, widths)
    return lax.slice_in_dim(padded, 1, length + 1, axis=along) - potential


def backward_diff(potential, along):
    length = potential.shape[along]
    widths = [(0, 0)] * potential.ndim
    widths[along] = (1, 0)
    padded = jnp.pad(potential, widths)
    return lax.slice_in_dim(padded, 0, length, axis=along) - potential


def curl_field(potential):
    part_one, part_two, part_three = potential[0], potential[1], potential[2]
    flux_one = forward_diff(part_three, 1) - forward_diff(part_two, 2)
    flux_two = forward_diff(part_one, 2) - forward_diff(part_three, 0)
    flux_three = forward_diff(part_two, 0) - forward_diff(part_one, 1)
    return jnp.stack([flux_one, flux_two, flux_three], axis=0)


def curl_back(field_h):
    back_one = backward_diff(field_h[1], 2) - backward_diff(field_h[2], 1)
    back_two = backward_diff(field_h[2], 0) - backward_diff(field_h[0], 2)
    back_three = backward_diff(field_h[0], 1) - backward_diff(field_h[1], 0)
    return jnp.stack([back_one, back_two, back_three], axis=0)


def material(density, region):
    iron_share = jnp.where(region == 0, density ** 3, jnp.zeros_like(density))
    iron_slope = jnp.where(region == 0, 3.0 * density ** 2, jnp.zeros_like(density))
    base_reluct = jnp.where(region == 1, magnet_reluct * jnp.ones_like(density), jnp.ones_like(density))
    return iron_share, iron_slope, base_reluct


def reference(state_hat, adjoint_hat, objective_hat, density, region):
    harm_table = harmonic_table()
    iron_share, iron_slope, base_reluct = material(density, region)

    def one_sample(carry, time_row):
        summed, gradient = carry
        state_time = jnp.tensordot(time_row, state_hat, axes=1, precision=lax.Precision.HIGHEST)
        adjoint_time = jnp.tensordot(time_row, adjoint_hat, axes=1, precision=lax.Precision.HIGHEST)
        state_flux = curl_field(state_time)
        adjoint_flux = curl_field(adjoint_time)
        flux_square = jnp.sum(state_flux * state_flux, axis=0)
        flux_inner = jnp.sum(state_flux * adjoint_flux, axis=0)
        iron_curve = iron_floor + (1.0 - iron_floor) * flux_square / (flux_square + saturation)
        curve_slope = (1.0 - iron_floor) * saturation / (flux_square + saturation) ** 2
        reluct_now = base_reluct + iron_share * (iron_curve - 1.0)
        reluct_slope = iron_share * curve_slope
        field_h = reluct_now[None] * adjoint_flux + (2.0 * reluct_slope * flux_inner)[None] * state_flux
        back_field = curl_back(field_h)
        summed = summed + (2.0 / NT) * time_row[:, None, None, None, None] * back_field[None]
        gradient = gradient + iron_slope * (iron_curve - 1.0) * flux_inner
        return (summed, gradient), time_row

    start_carry = (jnp.zeros(state_hat.shape, jnp.float32), jnp.zeros(density.shape, jnp.float32))
    finals, unused = lax.scan(one_sample, start_carry, harm_table)
    return objective_hat - finals[0], -finals[1] / NT
```

```python
import functools
import math

import jax
import jax.numpy as jnp
from jax import lax
from jax.experimental import pallas as pl
from jax.experimental.pallas import tpu as pltpu
from jax.sharding import PartitionSpec as P

NT = 40
magnet_reluct = 0.95
iron_floor = 0.05
saturation = 1.0
VMEM_LIMIT = 48 * 1024 * 1024


def passed_along(array, axis, by):
    size = lax.axis_size(axis)
    pairs = [(i, i + by) for i in range(size) if 0 <= i + by < size]
    return lax.ppermute(array, axis, pairs)


def angle(n, m, period):
    return 2.0 * math.pi * ((n * m) % period) / period


def weighted(terms):
    total = None
    for factor, value in terms:
        if abs(factor) < 1e-12:
            continue
        if abs(factor - 1.0) < 1e-12:
            total = value if total is None else total + value
        elif abs(factor + 1.0) < 1e-12:
            total = -value if total is None else total - value
        else:
            total = factor * value if total is None else total + factor * value
    return total


def add(a, b):
    return b if a is None else (a if b is None else a + b)


def sub(a, b):
    return a if b is None else (-b if a is None else a - b)


def synth(cos_of, sin_of, period):
    if period % 2:
        cos_part = {n: weighted([(math.cos(angle(n, m, period)), v) for m, v in cos_of.items()]) for n in range((period + 1) // 2)}
        sin_part = {n: weighted([(math.sin(angle(n, m, period)), v) for m, v in sin_of.items()]) for n in range((period + 1) // 2)}
        x = [None] * period
        for n in range((period + 1) // 2):
            x[n] = add(cos_part[n], sin_part[n])
            if n:
                x[period - n] = sub(cos_part[n], sin_part[n])
        return x
    half = period // 2
    odd = [None] * half
    cos_odd = {m: v for m, v in cos_of.items() if m % 2}
    sin_odd = {m: v for m, v in sin_of.items() if m % 2}
    for n in range(half // 2 + 1):
        c = weighted([(math.cos(angle(n, m, period)), v) for m, v in cos_odd.items()])
        s = weighted([(math.sin(angle(n, m, period)), v) for m, v in sin_odd.items()])
        odd[n] = add(c, s)
        if n and half - n != n:
            odd[half - n] = sub(s, c)
    cos_even = {m // 2: v for m, v in cos_of.items() if m % 2 == 0}
    sin_even = {m // 2: v for m, v in sin_of.items() if m % 2 == 0}
    if not cos_even:
        return [odd[n] for n in range(half)] + [sub(None, odd[n]) for n in range(half)]
    even = synth(cos_even, sin_even, half)
    return [add(even[n], odd[n]) for n in range(half)] + [sub(even[n], odd[n]) for n in range(half)]


def analyse(x, orders, period):
    if period % 2:
        plus = {n: (x[n] + x[period - n] if n else x[0]) for n in range((period + 1) // 2)}
        minus = {n: x[n] - x[period - n] for n in range(1, (period + 1) // 2)}
        cos_of = {m: weighted([(math.cos(angle(n, m, period)), v) for n, v in plus.items()]) for m in orders}
        sin_of = {m: weighted([(math.sin(angle(n, m, period)), v) for n, v in minus.items()]) for m in orders}
        return cos_of, sin_of
    half = period // 2
    odd = [x[n] - x[n + half] for n in range(half)]
    cos_in, sin_in = {}, {}
    for n in range(half // 2 + 1):
        if n and half - n != n:
            cos_in[n] = odd[n] - odd[half - n]
            sin_in[n] = odd[n] + odd[half - n]
        else:
            cos_in[n] = odd[n]
            sin_in[n] = odd[n]
    cos_of = {m: weighted([(math.cos(angle(n, m, period)), v) for n, v in cos_in.items()]) for m in orders if m % 2}
    sin_of = {m: weighted([(math.sin(angle(n, m, period)), v) for n, v in sin_in.items()]) for m in orders if m % 2}
    lower = [m // 2 for m in orders if m % 2 == 0]
    if lower:
        even = [x[n] + x[n + half] for n in range(half)]
        cos_even, sin_even = analyse(even, lower, half)
        cos_of.update({2 * m: v for m, v in cos_even.items()})
        sin_of.update({2 * m: v for m, v in sin_even.items()})
    return cos_of, sin_of


def lane_sum(rows, upward):
    width = rows.shape[1]
    source = lax.broadcasted_iota(jnp.int32, (2 * width, width), 0)
    source = jnp.where(source >= width, source - width, source)
    target = lax.broadcasted_iota(jnp.int32, (2 * width, width), 1)
    chosen = source >= target if upward else source <= target
    ones = jnp.where(chosen, 1.0, 0.0).astype(jnp.bfloat16)
    high = rows.astype(jnp.bfloat16)
    low = (rows - high.astype(jnp.float32)).astype(jnp.bfloat16)
    return jnp.dot(jnp.concatenate([high, low], axis=1), ones, preferred_element_type=jnp.float32)


def gauge_kernel(groups, state_ref, adjoint_ref, halo_ref, out_ref):
    planes, rows, width = state_ref.shape[2:]
    quarter = rows // groups
    for which, ref in enumerate((state_ref, adjoint_ref)):
        stacked = jnp.concatenate([ref[0, 2].reshape(planes * rows, width), halo_ref[which, 0, 1]], axis=0)
        phi = lane_sum(stacked, True).reshape(planes + 1, rows, width)
        last_row = lax.broadcasted_iota(jnp.int32, phi.shape, 1) == rows - 1
        phi_up = jnp.where(last_row, 0.0, pltpu.roll(phi, rows - 1, 1))
        p = ref[0, 0] + phi[1:] - phi[:-1]
        row_step = phi_up - phi
        q = ref[0, 1] + row_step[:-1]
        q_next = halo_ref[which, 0, 0] + row_step[planes]
        for d in range(groups):
            here = slice(d * quarter, (d + 1) * quarter)
            out_ref[d, 0, which, 0:planes] = p[:, here]
            out_ref[d, 0, which, planes : 2 * planes] = q[:, here]
            out_ref[d, 0, which, 2 * planes] = q_next[here]
            if d + 1 < groups:
                for i in range(planes):
                    out_ref[d, 0, which, 2 * planes + 1, i : i + 1] = p[i, (d + 1) * quarter : (d + 1) * quarter + 1]
            else:
                out_ref[d, 0, which, 2 * planes + 1] = jnp.zeros((quarter, width), jnp.float32)


def gauge(state_hat, adjoint_hat, halo, groups):
    coefs, parts, planes, rows, width = state_hat.shape
    quarter = rows // groups
    tiles = 2 * planes + 2
    block = pl.BlockSpec((1, parts, planes, rows, width), lambda c: (c, 0, 0, 0, 0))
    return pl.pallas_call(
        functools.partial(gauge_kernel, groups),
        grid=(coefs,),
        in_specs=[block, block, pl.BlockSpec((2, 1, 2, rows, width), lambda c: (0, c, 0, 0, 0))],
        out_specs=pl.BlockSpec((groups, 1, 2, tiles, quarter, width), lambda c: (0, c, 0, 0, 0, 0)),
        out_shape=jax.ShapeDtypeStruct((groups, coefs, 2, tiles, quarter, width), jnp.float32),
        compiler_params=pltpu.CompilerParams(vmem_limit_bytes=VMEM_LIMIT),
        name="gauge",
    )(state_hat, adjoint_hat, halo)


def sample_kernel(planes, me_ref, cells_ref, density_ref, region_ref, out_ref, grad_ref, time_ref, third_ref, psi_ref):
    coefs = cells_ref.shape[0]
    quarter, width = cells_ref.shape[3:]
    shape = (quarter, width)
    row = lax.broadcasted_iota(jnp.int32, shape, 0)
    lane = lax.broadcasted_iota(jnp.int32, shape, 1)
    last_lane = lane == width - 1
    last_row = row == quarter - 1
    first_row = row == 0
    my_rows = pl.ds(pl.multiple_of(me_ref[0] * quarter, quarter), quarter)
    orders = list(range(1, coefs // 2 + 1))
    psi_ref[...] = jnp.zeros(psi_ref.shape, jnp.float32)

    def next_lane(v):
        return jnp.where(last_lane, 0.0, pltpu.roll(v, width - 1, 1))

    def one_plane(i, carry):
        for which in range(2):
            for part in range(3):
                flux = []
                for c in range(coefs):
                    if part == 0:
                        q = cells_ref[c, which, planes + i]
                        flux.append(q - next_lane(q))
                    elif part == 1:
                        p = cells_ref[c, which, i]
                        flux.append(next_lane(p) - p)
                    else:
                        p = cells_ref[c, which, i]
                        edge = cells_ref[c, which, 2 * planes + 1, pl.ds(i, 1), :]
                        up = jnp.where(last_row, jnp.broadcast_to(edge, shape), pltpu.roll(p, quarter - 1, 0))
                        flux.append(cells_ref[c, which, planes + 1 + i] - cells_ref[c, which, planes + i] - (up - p))
                samples = synth({m: flux[2 * m - 2] for m in orders}, {m: flux[2 * m - 1] for m in orders}, NT)
                for n in range(NT):
                    time_ref[which * 3 + part, n] = samples[n]
        density = density_ref[i, my_rows]
        region = region_ref[i, my_rows]
        iron = region == 0
        share = jnp.where(iron, density * density * density, 0.0) * (1.0 - iron_floor)
        slope = jnp.where(iron, 3.0 * density * density, 0.0)
        base = jnp.where(region == 1, magnet_reluct, 1.0)
        total = jnp.zeros(shape, jnp.float32)
        for n in range(NT):
            b = [time_ref[j, n] for j in range(3)]
            a = [time_ref[3 + j, n] for j in range(3)]
            square = b[0] * b[0] + b[1] * b[1] + b[2] * b[2]
            inner = b[0] * a[0] + b[1] * a[1] + b[2] * a[2]
            inverse = 1.0 / (square + saturation)
            scaled = share * inverse
            reluct_now = base - scaled
            ratio = inverse * inner
            total = total + ratio
            along = scaled * ratio
            along = along + along
            for j in range(3):
                time_ref[j, n] = reluct_now * a[j] + along * b[j]
        grad_ref[i] = ((1.0 - iron_floor) / NT) * slope * total
        results = []
        for part in (2, 0, 1):
            x = [time_ref[part, n] for n in range(NT)]
            cos_of, sin_of = analyse(x, orders, NT)
            field = []
            for m in orders:
                field += [cos_of[m], sin_of[m]]
            if part == 2:
                for c in range(coefs):
                    third_ref[c] = field[c]
                psi = lane_sum(third_ref[...].reshape(coefs * quarter, width), False).reshape(coefs, quarter, width)
                third_ref[...] = psi
            elif part == 0:
                for c in range(coefs):
                    out_ref[c, i] = field[c] + (psi_ref[c] - third_ref[c])
            else:
                for c in range(coefs):
                    psi = third_ref[c]
                    down = jnp.where(first_row, 0.0, pltpu.roll(psi, 1, 0))
                    out_ref[c, planes + i] = field[c] + (down - psi)
                    out_ref[c, 2 * planes + 1, pl.ds(i, 1), :] = psi[quarter - 1 : quarter]
                    psi_ref[c] = psi
        return carry

    lax.fori_loop(0, planes, one_plane, 0)
    for c in range(coefs):
        out_ref[c, 2 * planes] = psi_ref[c]


def sample_fields(cells, density, region, planes):
    coefs, _, tiles, quarter, width = cells.shape
    me = lax.axis_index("sample").astype(jnp.int32).reshape(1)
    vmem = pl.BlockSpec(memory_space=pltpu.VMEM)
    return pl.pallas_call(
        functools.partial(sample_kernel, planes),
        in_specs=[pl.BlockSpec(memory_space=pltpu.SMEM), vmem, vmem, vmem],
        out_specs=[vmem, vmem],
        out_shape=[
            jax.ShapeDtypeStruct((coefs, tiles, quarter, width), jnp.float32),
            jax.ShapeDtypeStruct((planes, quarter, width), jnp.float32),
        ],
        scratch_shapes=[
            pltpu.VMEM((6, NT, quarter, width), jnp.float32),
            pltpu.VMEM((coefs, quarter, width), jnp.float32),
            pltpu.VMEM((coefs, quarter, width), jnp.float32),
        ],
        compiler_params=pltpu.CompilerParams(vmem_limit_bytes=VMEM_LIMIT),
        name="samples",
    )(me, cells, density, region)


def residual_kernel(fields_ref, halo_ref, objective_ref, out_ref):
    groups = fields_ref.shape[0]
    parts, planes, rows, width = objective_ref.shape[1:]
    quarter = rows // groups
    row = lax.broadcasted_iota(jnp.int32, (rows, width), 0)
    lane = lax.broadcasted_iota(jnp.int32, (rows, width), 1)

    def joined(ref, tile):
        return jnp.concatenate([ref[d, 0, tile] for d in range(groups)], axis=0)

    def with_edges(value, ref, tile, i):
        first = lax.broadcasted_iota(jnp.int32, (quarter, width), 0) == 0
        parts_of = [value[0:quarter]]
        for d in range(1, groups):
            edge = jnp.broadcast_to(ref[d - 1, 0, tile, i : i + 1, :], (quarter, width))
            parts_of.append(value[d * quarter : (d + 1) * quarter] + jnp.where(first, edge, 0.0))
        return jnp.concatenate(parts_of, axis=0)

    def lower_lane(v):
        return jnp.where(lane == 0, 0.0, pltpu.roll(v, 1, 1))

    before = with_edges(joined(halo_ref, 0), halo_ref, 2, planes - 1)
    for i in range(planes):
        h0 = joined(fields_ref, i)
        if i == 0:
            h0 = h0 + joined(halo_ref, 1)
        h1 = with_edges(joined(fields_ref, planes + i), fields_ref, 2 * planes + 1, i)
        out_ref[0, 0, i] = objective_ref[0, 0, i] - (2.0 / NT) * (lower_lane(h1) - h1)
        out_ref[0, 1, i] = objective_ref[0, 1, i] - (2.0 / NT) * (h0 - lower_lane(h0))
        lower_row = jnp.where(row == 0, 0.0, pltpu.roll(h0, 1, 0))
        out_ref[0, 2, i] = objective_ref[0, 2, i] - (2.0 / NT) * ((lower_row - h0) - (before - h1))
        before = h1


def residual(fields, halo, objective_hat):
    coefs, parts, planes, rows, width = objective_hat.shape
    groups, _, tiles, quarter, _ = fields.shape
    block = pl.BlockSpec((1, parts, planes, rows, width), lambda c: (c, 0, 0, 0, 0))
    return pl.pallas_call(
        residual_kernel,
        grid=(coefs,),
        in_specs=[
            pl.BlockSpec((groups, 1, tiles, quarter, width), lambda c: (0, c, 0, 0, 0)),
            pl.BlockSpec((groups, 1, 3, quarter, width), lambda c: (0, c, 0, 0, 0)),
            block,
        ],
        out_specs=block,
        out_shape=jax.ShapeDtypeStruct(objective_hat.shape, jnp.float32),
        compiler_params=pltpu.CompilerParams(vmem_limit_bytes=VMEM_LIMIT),
        name="residual",
    )(fields, halo, objective_hat)


def exchange(array):
    return lax.all_to_all(array, "sample", split_axis=0, concat_axis=0, tiled=True)


def local(state_hat, adjoint_hat, objective_hat, density, region):
    groups = lax.axis_size("sample")
    coefs, parts, planes, rows, width = state_hat.shape
    first = jnp.stack([state_hat[:, 1:3, 0], adjoint_hat[:, 1:3, 0]], axis=0)
    upper = passed_along(first, "space", -1)
    sent = gauge(state_hat, adjoint_hat, upper, groups)
    cells = exchange(sent).reshape((groups * coefs,) + sent.shape[2:])
    fields, density_gradient = sample_fields(cells, density, region, planes)
    back = exchange(fields.reshape((groups, coefs) + fields.shape[1:]))
    lower = passed_along(back[:, :, 2 * planes - 1 : 2 * planes + 2], "space", 1)
    return residual(back, lower, objective_hat), density_gradient


def solution(mesh):
    in_specs = (
        P("sample", None, "space", None, None),
        P("sample", None, "space", None, None),
        P("sample", None, "space", None, None),
        P("space", None, None),
        P("space", None, None),
    )
    out_specs = (P("sample", None, "space", None, None), P("space", "sample", None))
    return jax.shard_map(local, mesh=mesh, in_specs=in_specs, out_specs=out_specs, check_vma=False)
```

```python
import functools
import math

import jax
import jax.numpy as jnp
from jax import lax
from jax.experimental import pallas as pl
from jax.experimental.pallas import tpu as pltpu
from jax.sharding import PartitionSpec as P

NT = 40
magnet_reluct = 0.95
iron_floor = 0.05
saturation = 1.0
GAUGE_LIMIT = 16 * 1024 * 1024
SAMPLE_LIMIT = 16 * 1024 * 1024
RESIDUAL_LIMIT = 16 * 1024 * 1024


def passed_along(array, axis, by):
    size = lax.axis_size(axis)
    pairs = [(i, i + by) for i in range(size) if 0 <= i + by < size]
    return lax.ppermute(array, axis, pairs)


def angle(n, m, period):
    return 2.0 * math.pi * ((n * m) % period) / period


def weighted(terms):
    total = None
    for factor, value in terms:
        if abs(factor) < 1e-12:
            continue
        if abs(factor - 1.0) < 1e-12:
            total = value if total is None else total + value
        elif abs(factor + 1.0) < 1e-12:
            total = -value if total is None else total - value
        else:
            total = factor * value if total is None else total + factor * value
    return total


def add(a, b):
    return b if a is None else (a if b is None else a + b)


def sub(a, b):
    return a if b is None else (-b if a is None else a - b)


def synth(cos_of, sin_of, period):
    if period % 2:
        cos_part = {n: weighted([(math.cos(angle(n, m, period)), v) for m, v in cos_of.items()]) for n in range((period + 1) // 2)}
        sin_part = {n: weighted([(math.sin(angle(n, m, period)), v) for m, v in sin_of.items()]) for n in range((period + 1) // 2)}
        x = [None] * period
        for n in range((period + 1) // 2):
            x[n] = add(cos_part[n], sin_part[n])
            if n:
                x[period - n] = sub(cos_part[n], sin_part[n])
        return x
    half = period // 2
    odd = [None] * half
    cos_odd = {m: v for m, v in cos_of.items() if m % 2}
    sin_odd = {m: v for m, v in sin_of.items() if m % 2}
    for n in range(half // 2 + 1):
        c = weighted([(math.cos(angle(n, m, period)), v) for m, v in cos_odd.items()])
        s = weighted([(math.sin(angle(n, m, period)), v) for m, v in sin_odd.items()])
        odd[n] = add(c, s)
        if n and half - n != n:
            odd[half - n] = sub(s, c)
    cos_even = {m // 2: v for m, v in cos_of.items() if m % 2 == 0}
    sin_even = {m // 2: v for m, v in sin_of.items() if m % 2 == 0}
    if not cos_even:
        return [odd[n] for n in range(half)] + [sub(None, odd[n]) for n in range(half)]
    even = synth(cos_even, sin_even, half)
    return [add(even[n], odd[n]) for n in range(half)] + [sub(even[n], odd[n]) for n in range(half)]


def analyse(x, orders, period):
    if period % 2:
        plus = {n: (x[n] + x[period - n] if n else x[0]) for n in range((period + 1) // 2)}
        minus = {n: x[n] - x[period - n] for n in range(1, (period + 1) // 2)}
        cos_of = {m: weighted([(math.cos(angle(n, m, period)), v) for n, v in plus.items()]) for m in orders}
        sin_of = {m: weighted([(math.sin(angle(n, m, period)), v) for n, v in minus.items()]) for m in orders}
        return cos_of, sin_of
    half = period // 2
    odd = [x[n] - x[n + half] for n in range(half)]
    cos_in, sin_in = {}, {}
    for n in range(half // 2 + 1):
        if n and half - n != n:
            cos_in[n] = odd[n] - odd[half - n]
            sin_in[n] = odd[n] + odd[half - n]
        else:
            cos_in[n] = odd[n]
            sin_in[n] = odd[n]
    cos_of = {m: weighted([(math.cos(angle(n, m, period)), v) for n, v in cos_in.items()]) for m in orders if m % 2}
    sin_of = {m: weighted([(math.sin(angle(n, m, period)), v) for n, v in sin_in.items()]) for m in orders if m % 2}
    lower = [m // 2 for m in orders if m % 2 == 0]
    if lower:
        even = [x[n] + x[n + half] for n in range(half)]
        cos_even, sin_even = analyse(even, lower, half)
        cos_of.update({2 * m: v for m, v in cos_even.items()})
        sin_of.update({2 * m: v for m, v in sin_even.items()})
    return cos_of, sin_of


def lane_sum(rows, upward):
    width = rows.shape[1]
    source = lax.broadcasted_iota(jnp.int32, (2 * width, width), 0)
    source = jnp.where(source >= width, source - width, source)
    target = lax.broadcasted_iota(jnp.int32, (2 * width, width), 1)
    chosen = source >= target if upward else source <= target
    ones = jnp.where(chosen, 1.0, 0.0).astype(jnp.bfloat16)
    high = rows.astype(jnp.bfloat16)
    low = (rows - high.astype(jnp.float32)).astype(jnp.bfloat16)
    return jnp.dot(jnp.concatenate([high, low], axis=1), ones, preferred_element_type=jnp.float32)


def partner(me, r, groups):
    if groups & (groups - 1) == 0:
        return jnp.bitwise_xor(me, r)
    return lax.rem(me + r, groups)


def origin(me, r, groups):
    if groups & (groups - 1) == 0:
        return jnp.bitwise_xor(me, r)
    return lax.rem(me + groups - r, groups)


def exchange(messages):
    groups = len(messages)
    taken = [messages[0]] + [None] * (groups - 1)
    for r in list(range(2, groups)) + [1]:
        if groups & (groups - 1) == 0:
            pairs = [(i, i ^ r) for i in range(groups)]
        else:
            pairs = [(i, (i + r) % groups) for i in range(groups)]
        taken[r] = lax.ppermute(messages[r], "sample", pairs)
    return taken


def tiles_for(rows, quarter):
    return -(-rows // quarter)


VMEM = pl.BlockSpec(memory_space=pltpu.VMEM)
SMEM = pl.BlockSpec(memory_space=pltpu.SMEM)
HBM = pl.BlockSpec(memory_space=pltpu.HBM)


class Chunk:
    def __init__(self, kind, lo, hi):
        self.kind, self.lo, self.hi, self.n = kind, lo, hi, hi - lo
        self.q_from = 1 if kind == 1 else 0
        self.q_to = self.n if kind == 2 else self.n + 1
        self.nq = self.q_to - self.q_from
        self.h_from = 1 if kind == 0 else 0
        self.h_to = self.n + 1 if kind == 2 else self.n
        self.nh = self.h_to - self.h_from + (1 if kind == 1 else 0)

    def sent(self, coefs, quarter):
        return 2 * coefs * (self.n + self.nq) + tiles_for(2 * coefs * self.n, quarter)

    def back(self, coefs, quarter):
        return coefs * (self.nh + self.n) + tiles_for(coefs * self.n, quarter)


def gauge_kernel(chunk, groups, me_ref, state_ref, adjoint_ref, halo_ref, *rest):
    out_refs, (held, p_held, q_held, sems) = rest[:groups], rest[groups:]
    coefs, parts, planes, rows, width = state_ref.shape
    quarter = rows // groups
    n, nq = chunk.n, chunk.nq
    own = held.shape[3]
    me = me_ref[0]
    copies = []
    for c in range(coefs):
        for which, ref in enumerate((state_ref, adjoint_ref)):
            copy = pltpu.make_async_copy(ref.at[c, :, pl.ds(chunk.lo, own)], held.at[which, c], sems.at[which, c])
            copy.start()
            copies.append((c, which, copy))
    zero_rows = jnp.zeros((n, quarter, width), jnp.float32)
    last_row = lax.broadcasted_iota(jnp.int32, (n + 1, rows, width), 1) == rows - 1
    for c, which, copy in copies:
        copy.wait()
        third = held[which, c, 2]
        second = held[which, c, 1]
        if own == n:
            third = jnp.concatenate([third, halo_ref[which, c, 1][None]], axis=0)
            second = jnp.concatenate([second, halo_ref[which, c, 0][None]], axis=0)
        phi = lane_sum(third.reshape((n + 1) * rows, width), True).reshape(n + 1, rows, width)
        phi_up = jnp.where(last_row, 0.0, pltpu.roll(phi, rows - 1, 1))
        p_held[which, c, :, 0:rows] = held[which, c, 0, 0:n] + phi[1:] - phi[:-1]
        p_held[which, c, :, rows : rows + quarter] = zero_rows
        q_held[which, c] = (second + (phi_up - phi))[chunk.q_from : chunk.q_to]
        base = (which * coefs + c) * (n + nq)
        for r in range(groups):
            start = pl.multiple_of(partner(me, r, groups) * quarter, quarter)
            out_refs[r][base : base + n] = p_held[which, c, :, pl.ds(start, quarter)]
            out_refs[r][base + n : base + n + nq] = q_held[which, c, :, pl.ds(start, quarter)]
            for i in range(n):
                spot = (which * coefs + c) * n + i
                edge = p_held[which, c, i, pl.ds(pl.multiple_of(start + quarter, quarter), quarter)]
                tile = 2 * coefs * (n + nq) + spot // quarter
                out_refs[r][tile, spot % quarter : spot % quarter + 1] = edge[0:1]


def gauge(chunk, groups, me, state_hat, adjoint_hat, halo):
    coefs, parts, planes, rows, width = state_hat.shape
    quarter = rows // groups
    own = min(chunk.n + 1, planes - chunk.lo)
    shape = jax.ShapeDtypeStruct((chunk.sent(coefs, quarter), quarter, width), jnp.float32)
    return pl.pallas_call(
        functools.partial(gauge_kernel, chunk, groups),
        in_specs=[SMEM, HBM, HBM, VMEM],
        out_specs=[VMEM] * groups,
        out_shape=[shape] * groups,
        scratch_shapes=[
            pltpu.VMEM((2, coefs, parts, own, rows, width), jnp.float32),
            pltpu.VMEM((2, coefs, chunk.n, rows + quarter, width), jnp.float32),
            pltpu.VMEM((2, coefs, chunk.nq, rows, width), jnp.float32),
            pltpu.SemaphoreType.DMA((2, coefs)),
        ],
        compiler_params=pltpu.CompilerParams(vmem_limit_bytes=GAUGE_LIMIT),
        cost_estimate=pl.CostEstimate(flops=2 * 10**9, bytes_accessed=4 * 10**6, transcendentals=0),
        name="gauge%d" % chunk.kind,
    )(me, state_hat, adjoint_hat, halo)


def sample_kernel(chunk, groups, coefs, *refs):
    n, nq, kind = chunk.n, chunk.nq, chunk.kind
    me_ref, message_refs, refs = refs[0], refs[1 : 1 + groups], refs[1 + groups :]
    density_ref, region_ref, refs = refs[0], refs[1], refs[2:]
    edge_q_ref = edge_h_ref = None
    if kind:
        edge_q_ref, edge_h_ref, refs = refs[0], refs[1], refs[2:]
    out_refs, grad_ref, refs = refs[:groups], refs[groups], refs[groups + 1 :]
    if kind == 0:
        first_q_ref, last_q_ref, pending_ref, last_psi_ref = refs[:4]
        refs = refs[4:]
    p_ref, q_ref, edge_ref, time_ref, third_ref, psi_ref, h0_ref, h1_ref, tail_ref = refs
    quarter, width = p_ref.shape[4:]
    shape = (quarter, width)
    me = me_ref[0]
    row = lax.broadcasted_iota(jnp.int32, shape, 0)
    lane = lax.broadcasted_iota(jnp.int32, shape, 1)
    last_lane = lane == width - 1
    last_row = row == quarter - 1
    first_row = row == 0
    my_rows = pl.ds(pl.multiple_of(me * quarter, quarter), quarter)
    total_coefs = groups * coefs
    orders = list(range(1, total_coefs // 2 + 1))
    place = [(c // coefs, c % coefs) for c in range(total_coefs)]

    for r in range(groups):
        g = origin(me, r, groups)
        for which in range(2):
            for c in range(coefs):
                base = (which * coefs + c) * (n + nq)
                p_ref[which, g, c] = message_refs[r][base : base + n]
                q_ref[which, g, c, chunk.q_from : chunk.q_to] = message_refs[r][base + n : base + n + nq]
        for t in range(tiles_for(2 * coefs * n, quarter)):
            edge_ref[g, t * quarter : (t + 1) * quarter] = message_refs[r][2 * coefs * (n + nq) + t]
    for which in range(2):
        for g in range(groups):
            for c in range(coefs):
                if kind == 0:
                    first_q_ref[which, g, c] = q_ref[which, g, c, 0]
                    last_q_ref[which, g, c] = q_ref[which, g, c, n]
                elif kind == 1:
                    q_ref[which, g, c, 0] = edge_q_ref[which, g, c]
                else:
                    q_ref[which, g, c, n] = edge_q_ref[which, g, c]
    if kind == 1:
        psi_ref[...] = edge_h_ref[...]
    else:
        psi_ref[...] = jnp.zeros(psi_ref.shape, jnp.float32)

    def next_lane(v):
        return jnp.where(last_lane, 0.0, pltpu.roll(v, width - 1, 1))

    def one_plane(i, carry):
        for which in range(2):
            for part in range(3):
                flux = []
                for g, c in place:
                    if part == 0:
                        q = q_ref[which, g, c, i]
                        flux.append(q - next_lane(q))
                    elif part == 1:
                        p = p_ref[which, g, c, i]
                        flux.append(next_lane(p) - p)
                    else:
                        p = p_ref[which, g, c, i]
                        edge = edge_ref[g, pl.ds((which * coefs + c) * n + i, 1), :]
                        up = jnp.where(last_row, jnp.broadcast_to(edge, shape), pltpu.roll(p, quarter - 1, 0))
                        flux.append(q_ref[which, g, c, i + 1] - q_ref[which, g, c, i] - (up - p))
                samples = synth({m: flux[2 * m - 2] for m in orders}, {m: flux[2 * m - 1] for m in orders}, NT)
                for k in range(NT):
                    time_ref[which * 3 + part, k] = samples[k]
        density = density_ref[chunk.lo + i, my_rows]
        region = region_ref[chunk.lo + i, my_rows]
        iron = region == 0
        share = jnp.where(iron, density * density * density, 0.0) * (1.0 - iron_floor)
        slope = jnp.where(iron, 3.0 * density * density, 0.0)
        base = jnp.where(region == 1, magnet_reluct, 1.0)
        total = jnp.zeros(shape, jnp.float32)
        for k in range(NT):
            b = [time_ref[j, k] for j in range(3)]
            a = [time_ref[3 + j, k] for j in range(3)]
            square = b[0] * b[0] + b[1] * b[1] + b[2] * b[2]
            inner = b[0] * a[0] + b[1] * a[1] + b[2] * a[2]
            inverse = 1.0 / (square + saturation)
            scaled = share * inverse
            reluct_now = base - scaled
            ratio = inverse * inner
            total = total + ratio
            along = scaled * ratio
            along = along + along
            for j in range(3):
                time_ref[j, k] = reluct_now * a[j] + along * b[j]
        grad_ref[i] = ((1.0 - iron_floor) / NT) * slope * total
        for part in (2, 0, 1):
            cos_of, sin_of = analyse([time_ref[part, k] for k in range(NT)], orders, NT)
            field = []
            for m in orders:
                field += [cos_of[m], sin_of[m]]
            if part == 2:
                for at in range(total_coefs):
                    third_ref[at] = field[at]
                psi = lane_sum(third_ref[...].reshape(total_coefs * quarter, width), False)
                third_ref[...] = psi.reshape(total_coefs, quarter, width)
            elif part == 0:
                for at, (g, c) in enumerate(place):
                    h0_ref[g, c, i] = field[at] + (psi_ref[g, c] - third_ref[at])
            else:
                for at, (g, c) in enumerate(place):
                    psi = third_ref[at]
                    down = jnp.where(first_row, 0.0, pltpu.roll(psi, 1, 0))
                    h1_ref[g, c, i] = field[at] + (down - psi)
                    tail_ref[g, pl.ds(c * n + i, 1), :] = psi[quarter - 1 : quarter]
                    psi_ref[g, c] = psi
        return carry

    lax.fori_loop(0, n, one_plane, 0)
    for g, c in place:
        if kind == 0:
            pending_ref[g, c] = h0_ref[g, c, 0]
            last_psi_ref[g, c] = psi_ref[g, c]
        elif kind == 1:
            h0_ref[g, c, n] = psi_ref[g, c]
        else:
            h0_ref[g, c, n] = edge_h_ref[g, c] + psi_ref[g, c]
    step = chunk.nh + n
    for r in range(groups):
        g = partner(me, r, groups)
        for c in range(coefs):
            out_refs[r][c * step : c * step + chunk.nh] = h0_ref[g, c, chunk.h_from : chunk.h_from + chunk.nh]
            out_refs[r][c * step + chunk.nh : (c + 1) * step] = h1_ref[g, c]
        for t in range(tiles_for(coefs * n, quarter)):
            out_refs[r][coefs * step + t] = tail_ref[g, t * quarter : (t + 1) * quarter]


def sample_fields(chunk, me, messages, density, region, coefs, edges):
    groups = len(messages)
    _, quarter, width = messages[0].shape
    n = chunk.n
    f32 = jnp.float32
    shapes = [jax.ShapeDtypeStruct((chunk.back(coefs, quarter), quarter, width), f32)] * groups
    shapes.append(jax.ShapeDtypeStruct((n, quarter, width), f32))
    if chunk.kind == 0:
        shapes += [jax.ShapeDtypeStruct((2, groups, coefs, quarter, width), f32)] * 2
        shapes += [jax.ShapeDtypeStruct((groups, coefs, quarter, width), f32)] * 2
    operands = [me, *messages, density, region, *edges]
    return pl.pallas_call(
        functools.partial(sample_kernel, chunk, groups, coefs),
        in_specs=[SMEM] + [VMEM] * (len(operands) - 1),
        out_specs=[VMEM] * len(shapes),
        out_shape=shapes,
        scratch_shapes=[
            pltpu.VMEM((2, groups, coefs, n, quarter, width), f32),
            pltpu.VMEM((2, groups, coefs, n + 1, quarter, width), f32),
            pltpu.VMEM((groups, tiles_for(2 * coefs * n, quarter) * quarter, width), f32),
            pltpu.VMEM((6, NT, quarter, width), f32),
            pltpu.VMEM((groups * coefs, quarter, width), f32),
            pltpu.VMEM((groups, coefs, quarter, width), f32),
            pltpu.VMEM((groups, coefs, n + 1, quarter, width), f32),
            pltpu.VMEM((groups, coefs, n, quarter, width), f32),
            pltpu.VMEM((groups, tiles_for(coefs * n, quarter) * quarter, width), f32),
        ],
        compiler_params=pltpu.CompilerParams(vmem_limit_bytes=SAMPLE_LIMIT),
        cost_estimate=pl.CostEstimate(flops=3 * 10**9, bytes_accessed=8 * 10**6, transcendentals=0),
        name="samples%d" % chunk.kind,
    )(*operands)


def last_plane_kernel(chunk, coefs, me_ref, *refs):
    groups = len(refs) - 2
    message_refs, out_ref, row_ref = refs[:groups], refs[groups], refs[groups + 1]
    quarter, width = message_refs[0].shape[1:]
    rows = quarter * groups
    step = chunk.nh + chunk.n
    me = me_ref[0]
    for c in range(coefs):
        for r in range(groups):
            here = pl.ds(pl.multiple_of(origin(me, r, groups) * quarter, quarter), quarter)
            row_ref[c, here] = message_refs[r][(c + 1) * step - 1]
            out_ref[c, 1, here] = message_refs[r][c * step + chunk.nh - 1]
        for r in range(groups):
            add_edge(row_ref.at[c], message_refs[r], chunk, coefs, c * chunk.n + chunk.n - 1, origin(me, r, groups) * quarter + quarter)
        out_ref[c, 0] = row_ref[c, 0:rows]


def add_edge(target, message_ref, chunk, coefs, spot, row):
    quarter = message_ref.shape[1]
    tile = coefs * (chunk.nh + chunk.n) + spot // quarter
    here = pl.ds(pl.multiple_of(row, quarter), 1)
    target[here] = target[here] + message_ref[tile, spot % quarter : spot % quarter + 1]


def last_plane(chunk, me, messages, coefs):
    groups = len(messages)
    _, quarter, width = messages[0].shape
    rows = groups * quarter
    return pl.pallas_call(
        functools.partial(last_plane_kernel, chunk, coefs),
        in_specs=[SMEM] + [VMEM] * groups,
        out_specs=VMEM,
        out_shape=jax.ShapeDtypeStruct((coefs, 2, rows, width), jnp.float32),
        scratch_shapes=[pltpu.VMEM((coefs, rows + quarter, width), jnp.float32)],
        name="last_plane",
    )(me, *messages)


def residual_kernel(chunks, groups, coefs, me_ref, *refs):
    message_refs = [refs[k * groups : (k + 1) * groups] for k in range(len(chunks))]
    halo_ref, objective_ref, out_ref, h0_ref, h1_ref = refs[len(chunks) * groups :]
    parts, planes, rows, width = objective_ref.shape[1:]
    quarter = rows // groups
    me = me_ref[0]
    row = lax.broadcasted_iota(jnp.int32, (rows, width), 0)
    lane = lax.broadcasted_iota(jnp.int32, (rows, width), 1)

    def lower_lane(v):
        return jnp.where(lane == 0, 0.0, pltpu.roll(v, 1, 1))

    def one_coef(c):
        for chunk, messages in zip(chunks, message_refs):
            n = chunk.n
            step = chunk.nh + n
            for r in range(groups):
                g = origin(me, r, groups)
                here = pl.ds(pl.multiple_of(g * quarter, quarter), quarter)
                count = chunk.h_to - chunk.h_from
                h0_ref[chunk.lo + chunk.h_from : chunk.lo + chunk.h_to, here] = messages[r][c * step : c * step + count]
                h1_ref[chunk.lo : chunk.hi, here] = messages[r][c * step + chunk.nh : (c + 1) * step]
            for r in range(groups):
                g = origin(me, r, groups)
                for i in range(n):
                    add_edge(h1_ref.at[chunk.lo + i], messages[r], chunk, coefs, c * n + i, g * quarter + quarter)
        before = halo_ref[c, 0]
        for i in range(planes):
            h0 = h0_ref[i]
            if i == 0:
                h0 = h0 + halo_ref[c, 1]
            h1 = h1_ref[i, 0:rows]
            out_ref[0, 0, i] = objective_ref[0, 0, i] - (2.0 / NT) * (lower_lane(h1) - h1)
            out_ref[0, 1, i] = objective_ref[0, 1, i] - (2.0 / NT) * (h0 - lower_lane(h0))
            lower_row = jnp.where(row == 0, 0.0, pltpu.roll(h0, 1, 0))
            out_ref[0, 2, i] = objective_ref[0, 2, i] - (2.0 / NT) * ((lower_row - h0) - (before - h1))
            before = h1

    for c in range(coefs):
        pl.when(pl.program_id(0) == c)(functools.partial(one_coef, c))


def residual(chunks, me, returned, halo, objective_hat):
    coefs, parts, planes, rows, width = objective_hat.shape
    groups = len(returned[0])
    quarter = rows // groups
    block = pl.BlockSpec((1, parts, planes, rows, width), lambda c: (c, 0, 0, 0, 0))
    operands = [m for messages in returned for m in messages]
    return pl.pallas_call(
        functools.partial(residual_kernel, chunks, groups, coefs),
        grid=(coefs,),
        in_specs=[SMEM] + [VMEM] * (len(operands) + 1) + [block],
        out_specs=block,
        out_shape=jax.ShapeDtypeStruct(objective_hat.shape, jnp.float32),
        scratch_shapes=[
            pltpu.VMEM((planes, rows, width), jnp.float32),
            pltpu.VMEM((planes, rows + quarter, width), jnp.float32),
        ],
        compiler_params=pltpu.CompilerParams(vmem_limit_bytes=RESIDUAL_LIMIT),
        name="residual",
    )(me, *operands, halo, objective_hat)


def local(state_hat, adjoint_hat, objective_hat, density, region):
    groups = lax.axis_size("sample")
    coefs, parts, planes, rows, width = state_hat.shape
    me = lax.axis_index("sample").astype(jnp.int32).reshape(1)
    first = planes // 4
    last = first + (planes - first) // 2
    middle_chunk, last_chunk, first_chunk = Chunk(0, first, last), Chunk(1, last, planes), Chunk(2, 0, first)
    upper = passed_along(jnp.stack([state_hat[:, 1:3, 0], adjoint_hat[:, 1:3, 0]], axis=0), "space", -1)
    sent0 = gauge(middle_chunk, groups, me, state_hat, adjoint_hat, jnp.zeros((8, 128), jnp.float32))
    cells0 = exchange(sent0)
    sent1 = gauge(last_chunk, groups, me, state_hat, adjoint_hat, upper)
    cells1 = exchange(sent1)
    sent2 = gauge(first_chunk, groups, me, state_hat, adjoint_hat, upper)
    cells2 = exchange(sent2)
    *out0, grad0, first_q, last_q, pending, last_psi = sample_fields(middle_chunk, me, cells0, density, region, coefs, ())
    back0 = exchange(out0)
    *out1, grad1 = sample_fields(last_chunk, me, cells1, density, region, coefs, (last_q, last_psi))
    back1 = exchange(out1)
    *out2, grad2 = sample_fields(first_chunk, me, cells2, density, region, coefs, (first_q, pending))
    back2 = exchange(out2)
    lower = passed_along(last_plane(last_chunk, me, back1, coefs), "space", 1)
    adjoint_residual = residual((middle_chunk, last_chunk, first_chunk), me, (back0, back1, back2), lower, objective_hat)
    return adjoint_residual, jnp.concatenate([grad2, grad0, grad1], axis=0)


def solution(mesh):
    in_specs = (
        P("sample", None, "space", None, None),
        P("sample", None, "space", None, None),
        P("sample", None, "space", None, None),
        P("space", None, None),
        P("space", None, None),
    )
    out_specs = (P("sample", None, "space", None, None), P("space", "sample", None))
    return jax.shard_map(local, mesh=mesh, in_specs=in_specs, out_specs=out_specs, check_vma=False)
```

```python
import functools
import math

import jax
import jax.numpy as jnp
from jax import lax
from jax.experimental import pallas as pl
from jax.experimental.pallas import tpu as pltpu
from jax.sharding import PartitionSpec as P

NT = 40
magnet_reluct = 0.95
iron_floor = 0.05
saturation = 1.0
GAUGE_LIMIT = 16 * 1024 * 1024
FIRST_LIMIT = 62 * 1024 * 1024
SAMPLE_LIMIT = 16 * 1024 * 1024
RESIDUAL_LIMIT = 16 * 1024 * 1024


def passed_along(array, axis, by):
    size = lax.axis_size(axis)
    pairs = [(i, i + by) for i in range(size) if 0 <= i + by < size]
    return lax.ppermute(array, axis, pairs)


def angle(n, m, period):
    return 2.0 * math.pi * ((n * m) % period) / period


def weighted(terms):
    total = None
    for factor, value in terms:
        if abs(factor) < 1e-12:
            continue
        if abs(factor - 1.0) < 1e-12:
            total = value if total is None else total + value
        elif abs(factor + 1.0) < 1e-12:
            total = -value if total is None else total - value
        else:
            total = factor * value if total is None else total + factor * value
    return total


def add(a, b):
    return b if a is None else (a if b is None else a + b)


def sub(a, b):
    return a if b is None else (-b if a is None else a - b)


def synth(cos_of, sin_of, period):
    if period % 2:
        cos_part = {n: weighted([(math.cos(angle(n, m, period)), v) for m, v in cos_of.items()]) for n in range((period + 1) // 2)}
        sin_part = {n: weighted([(math.sin(angle(n, m, period)), v) for m, v in sin_of.items()]) for n in range((period + 1) // 2)}
        x = [None] * period
        for n in range((period + 1) // 2):
            x[n] = add(cos_part[n], sin_part[n])
            if n:
                x[period - n] = sub(cos_part[n], sin_part[n])
        return x
    half = period // 2
    odd = [None] * half
    cos_odd = {m: v for m, v in cos_of.items() if m % 2}
    sin_odd = {m: v for m, v in sin_of.items() if m % 2}
    for n in range(half // 2 + 1):
        c = weighted([(math.cos(angle(n, m, period)), v) for m, v in cos_odd.items()])
        s = weighted([(math.sin(angle(n, m, period)), v) for m, v in sin_odd.items()])
        odd[n] = add(c, s)
        if n and half - n != n:
            odd[half - n] = sub(s, c)
    cos_even = {m // 2: v for m, v in cos_of.items() if m % 2 == 0}
    sin_even = {m // 2: v for m, v in sin_of.items() if m % 2 == 0}
    if not cos_even:
        return [odd[n] for n in range(half)] + [sub(None, odd[n]) for n in range(half)]
    even = synth(cos_even, sin_even, half)
    return [add(even[n], odd[n]) for n in range(half)] + [sub(even[n], odd[n]) for n in range(half)]


def analyse(x, orders, period):
    if period % 2:
        plus = {n: (x[n] + x[period - n] if n else x[0]) for n in range((period + 1) // 2)}
        minus = {n: x[n] - x[period - n] for n in range(1, (period + 1) // 2)}
        cos_of = {m: weighted([(math.cos(angle(n, m, period)), v) for n, v in plus.items()]) for m in orders}
        sin_of = {m: weighted([(math.sin(angle(n, m, period)), v) for n, v in minus.items()]) for m in orders}
        return cos_of, sin_of
    half = period // 2
    odd = [x[n] - x[n + half] for n in range(half)]
    cos_in, sin_in = {}, {}
    for n in range(half // 2 + 1):
        if n and half - n != n:
            cos_in[n] = odd[n] - odd[half - n]
            sin_in[n] = odd[n] + odd[half - n]
        else:
            cos_in[n] = odd[n]
            sin_in[n] = odd[n]
    cos_of = {m: weighted([(math.cos(angle(n, m, period)), v) for n, v in cos_in.items()]) for m in orders if m % 2}
    sin_of = {m: weighted([(math.sin(angle(n, m, period)), v) for n, v in sin_in.items()]) for m in orders if m % 2}
    lower = [m // 2 for m in orders if m % 2 == 0]
    if lower:
        even = [x[n] + x[n + half] for n in range(half)]
        cos_even, sin_even = analyse(even, lower, half)
        cos_of.update({2 * m: v for m, v in cos_even.items()})
        sin_of.update({2 * m: v for m, v in sin_even.items()})
    return cos_of, sin_of


def lane_sum(rows, upward):
    width = rows.shape[1]
    source = lax.broadcasted_iota(jnp.int32, (2 * width, width), 0)
    source = jnp.where(source >= width, source - width, source)
    target = lax.broadcasted_iota(jnp.int32, (2 * width, width), 1)
    chosen = source >= target if upward else source <= target
    ones = jnp.where(chosen, 1.0, 0.0).astype(jnp.bfloat16)
    high = rows.astype(jnp.bfloat16)
    low = (rows - high.astype(jnp.float32)).astype(jnp.bfloat16)
    return jnp.dot(jnp.concatenate([high, low], axis=1), ones, preferred_element_type=jnp.float32)


def partner(me, r, groups):
    if groups & (groups - 1) == 0:
        return jnp.bitwise_xor(me, r)
    return lax.rem(me + r, groups)


def origin(me, r, groups):
    if groups & (groups - 1) == 0:
        return jnp.bitwise_xor(me, r)
    return lax.rem(me + groups - r, groups)


def exchange(messages):
    groups = len(messages)
    taken = [messages[0]] + [None] * (groups - 1)
    for r in list(range(2, groups)) + [1]:
        if groups & (groups - 1) == 0:
            pairs = [(i, i ^ r) for i in range(groups)]
        else:
            pairs = [(i, (i + r) % groups) for i in range(groups)]
        taken[r] = lax.ppermute(messages[r], "sample", pairs)
    return taken


def tiles_for(rows, quarter):
    return -(-rows // quarter)


VMEM = pl.BlockSpec(memory_space=pltpu.VMEM)
SMEM = pl.BlockSpec(memory_space=pltpu.SMEM)
HBM = pl.BlockSpec(memory_space=pltpu.HBM)
ANY = pl.BlockSpec(memory_space=pl.ANY)
LITTLE = pl.CostEstimate(flops=1000, bytes_accessed=1000, transcendentals=0)


class Chunk:
    def __init__(self, kind, lo, hi, at=0):
        self.at = at
        self.kind, self.lo, self.hi, self.n = kind, lo, hi, hi - lo
        self.q_from = 1 if kind == 1 else 0
        self.q_to = self.n if kind == 2 else self.n + 1
        self.nq = self.q_to - self.q_from
        self.h_from = 1 if kind == 0 else 0
        self.h_to = self.n + 1 if kind == 2 else self.n
        self.nh = self.h_to - self.h_from + (1 if kind == 1 else 0)

    def sent(self, coefs, quarter):
        return 2 * coefs * (self.n + self.nq) + tiles_for(2 * coefs * self.n, quarter)

    def back(self, coefs, quarter):
        return coefs * (self.nh + self.n) + tiles_for(coefs * self.n, quarter)


def gauge_kernel(chunks, groups, has_halo, me_ref, state_ref, adjoint_ref, *rest):
    if has_halo:
        halo_ref, rest = rest[0], rest[1:]
    out_refs, rest = rest[:groups], rest[groups:]
    if not has_halo:
        first_ref, first_sems = rest[0], rest[-1]
        rest = rest[1:-1]
    coefs, parts, planes, rows, width = state_ref.shape
    quarter = rows // groups
    me = me_ref[0]
    sources = (state_ref, adjoint_ref)
    copies = {}
    for which in range(2):
        for at, chunk in enumerate(chunks):
            held, sems = rest[5 * at], rest[5 * at + 4]
            planes_here = pl.ds(chunk.lo, held.shape[3])
            for c in range(coefs):
                copy = pltpu.make_async_copy(sources[which].at[c, :, planes_here], held.at[which, c], sems.at[which, c])
                copy.start()
                copies[which, at, c] = copy
    firsts = []
    if not has_halo:
        for which in range(2):
            for c in range(coefs):
                source = sources[which].at[c, pl.ds(1, 2), 0]
                firsts.append(pltpu.make_async_copy(source, first_ref.at[which, c], first_sems.at[which, c]))
                firsts[-1].start()
    for which in range(2):
        for at, chunk in enumerate(chunks):
            held, phi_held, p_held, q_held, _ = rest[5 * at : 5 * at + 5]
            n, nq = chunk.n, chunk.nq
            own = held.shape[3]
            last_row = lax.broadcasted_iota(jnp.int32, (n + 1, rows, width), 1) == rows - 1
            zero_rows = jnp.zeros((n, quarter, width), jnp.float32)
            for c in range(coefs):
                copies[which, at, c].wait()
            third = held[which, :, 2]
            if own == n:
                third = jnp.concatenate([third, halo_ref[which, :, 1][:, None]], axis=1)
            phi_all = lane_sum(third.reshape(coefs * (n + 1) * rows, width), True)
            phi_held[...] = phi_all.reshape(coefs, n + 1, rows, width)
            for c in range(coefs):
                second = held[which, c, 1]
                if own == n:
                    second = jnp.concatenate([second, halo_ref[which, c, 0][None]], axis=0)
                phi = phi_held[c]
                phi_up = jnp.where(last_row, 0.0, pltpu.roll(phi, rows - 1, 1))
                p_held[which, c, :, 0:rows] = held[which, c, 0, 0:n] + phi[1:] - phi[:-1]
                p_held[which, c, :, rows : rows + quarter] = zero_rows
                q_held[which, c] = (second + (phi_up - phi))[chunk.q_from : chunk.q_to]
            for c in range(coefs):
                base = chunk.at + (which * coefs + c) * (n + nq)
                for r in range(groups):
                    start = pl.multiple_of(partner(me, r, groups) * quarter, quarter)
                    out_refs[r][base : base + n] = p_held[which, c, :, pl.ds(start, quarter)]
                    out_refs[r][base + n : base + n + nq] = q_held[which, c, :, pl.ds(start, quarter)]
                    for i in range(n):
                        spot = (which * coefs + c) * n + i
                        edge = p_held[which, c, i, pl.ds(pl.multiple_of(start + quarter, quarter), quarter)]
                        tile = chunk.at + 2 * coefs * (n + nq) + spot // quarter
                        out_refs[r][tile, spot % quarter : spot % quarter + 1] = edge[0:1]
    for copy in firsts:
        copy.wait()


def gauge(chunks, groups, me, state_hat, adjoint_hat, halo=None):
    coefs, parts, planes, rows, width = state_hat.shape
    quarter = rows // groups
    tiles = sum(chunk.sent(coefs, quarter) for chunk in chunks)
    shapes = [jax.ShapeDtypeStruct((tiles, quarter, width), jnp.float32)] * groups
    scratch = []
    for chunk in chunks:
        own = min(chunk.n + 1, planes - chunk.lo)
        scratch += [
            pltpu.VMEM((2, coefs, parts, own, rows, width), jnp.float32),
            pltpu.VMEM((coefs, chunk.n + 1, rows, width), jnp.float32),
            pltpu.VMEM((2, coefs, chunk.n, rows + quarter, width), jnp.float32),
            pltpu.VMEM((2, coefs, chunk.nq, rows, width), jnp.float32),
            pltpu.SemaphoreType.DMA((2, coefs)),
        ]
    operands, specs = [me, state_hat, adjoint_hat], [SMEM, HBM, HBM]
    if halo is None:
        shapes.append(jax.ShapeDtypeStruct((2, coefs, 2, rows, width), jnp.float32))
        scratch.append(pltpu.SemaphoreType.DMA((2, coefs)))
    else:
        operands.append(halo)
        specs.append(VMEM)
    return pl.pallas_call(
        functools.partial(gauge_kernel, chunks, groups, halo is not None),
        in_specs=specs,
        out_specs=[VMEM] * len(shapes),
        out_shape=shapes,
        scratch_shapes=scratch,
        compiler_params=pltpu.CompilerParams(vmem_limit_bytes=FIRST_LIMIT if halo is None else GAUGE_LIMIT),
        cost_estimate=LITTLE,
        name="gauge_middle" if halo is None else "gauge_ends",
    )(*operands)


def sample_kernel(chunk, groups, coefs, later, *refs):
    n, nq, kind = chunk.n, chunk.nq, chunk.kind
    me_ref, message_refs, refs = refs[0], refs[1 : 1 + groups], refs[1 + groups :]
    density_ref, region_ref, refs = refs[0], refs[1], refs[2:]
    edge_q_ref = edge_h_ref = None
    if kind:
        edge_q_ref, edge_h_ref, refs = refs[0], refs[1], refs[2:]
    refs = refs[later:]
    out_refs, grad_ref, refs = refs[:groups], refs[groups], refs[groups + 1 :]
    if kind == 0:
        first_q_ref, last_q_ref, pending_ref, last_psi_ref = refs[:4]
        refs = refs[4:]
    p_ref, q_ref, edge_ref, time_ref, third_ref, psi_ref, h0_ref, h1_ref, tail_ref = refs
    quarter, width = p_ref.shape[4:]
    shape = (quarter, width)
    me = me_ref[0]
    row = lax.broadcasted_iota(jnp.int32, shape, 0)
    lane = lax.broadcasted_iota(jnp.int32, shape, 1)
    last_lane = lane == width - 1
    last_row = row == quarter - 1
    first_row = row == 0
    my_rows = pl.ds(pl.multiple_of(me * quarter, quarter), quarter)
    total_coefs = groups * coefs
    orders = list(range(1, total_coefs // 2 + 1))
    place = [(c // coefs, c % coefs) for c in range(total_coefs)]

    for r in range(groups):
        g = origin(me, r, groups)
        for which in range(2):
            for c in range(coefs):
                base = chunk.at + (which * coefs + c) * (n + nq)
                p_ref[which, g, c] = message_refs[r][base : base + n]
                q_ref[which, g, c, chunk.q_from : chunk.q_to] = message_refs[r][base + n : base + n + nq]
        for t in range(tiles_for(2 * coefs * n, quarter)):
            edge_ref[g, t * quarter : (t + 1) * quarter] = message_refs[r][chunk.at + 2 * coefs * (n + nq) + t]
    for which in range(2):
        for g in range(groups):
            for c in range(coefs):
                if kind == 0:
                    first_q_ref[which, g, c] = q_ref[which, g, c, 0]
                    last_q_ref[which, g, c] = q_ref[which, g, c, n]
                elif kind == 1:
                    q_ref[which, g, c, 0] = edge_q_ref[which, g, c]
                else:
                    q_ref[which, g, c, n] = edge_q_ref[which, g, c]
    if kind == 1:
        psi_ref[...] = edge_h_ref[...]
    else:
        psi_ref[...] = jnp.zeros(psi_ref.shape, jnp.float32)

    def next_lane(v):
        return jnp.where(last_lane, 0.0, pltpu.roll(v, width - 1, 1))

    def one_plane(i, carry):
        for which in range(2):
            for part in range(3):
                flux = []
                for g, c in place:
                    if part == 0:
                        q = q_ref[which, g, c, i]
                        flux.append(q - next_lane(q))
                    elif part == 1:
                        p = p_ref[which, g, c, i]
                        flux.append(next_lane(p) - p)
                    else:
                        p = p_ref[which, g, c, i]
                        edge = edge_ref[g, pl.ds((which * coefs + c) * n + i, 1), :]
                        up = jnp.where(last_row, jnp.broadcast_to(edge, shape), pltpu.roll(p, quarter - 1, 0))
                        flux.append(q_ref[which, g, c, i + 1] - q_ref[which, g, c, i] - (up - p))
                samples = synth({m: flux[2 * m - 2] for m in orders}, {m: flux[2 * m - 1] for m in orders}, NT)
                for k in range(NT):
                    time_ref[which * 3 + part, k] = samples[k]
        density = density_ref[chunk.lo + i, my_rows]
        region = region_ref[chunk.lo + i, my_rows]
        iron = region == 0
        share = jnp.where(iron, density * density * density, 0.0) * (1.0 - iron_floor)
        slope = jnp.where(iron, 3.0 * density * density, 0.0)
        base = jnp.where(region == 1, magnet_reluct, 1.0)
        total = jnp.zeros(shape, jnp.float32)
        for k in range(NT):
            b = [time_ref[j, k] for j in range(3)]
            a = [time_ref[3 + j, k] for j in range(3)]
            square = b[0] * b[0] + b[1] * b[1] + b[2] * b[2]
            inner = b[0] * a[0] + b[1] * a[1] + b[2] * a[2]
            inverse = 1.0 / (square + saturation)
            scaled = share * inverse
            reluct_now = base - scaled
            ratio = inverse * inner
            total = total + ratio
            along = scaled * ratio
            along = along + along
            for j in range(3):
                time_ref[j, k] = reluct_now * a[j] + along * b[j]
        grad_ref[i] = ((1.0 - iron_floor) / NT) * slope * total
        for part in (2, 0, 1):
            cos_of, sin_of = analyse([time_ref[part, k] for k in range(NT)], orders, NT)
            field = []
            for m in orders:
                field += [cos_of[m], sin_of[m]]
            if part == 2:
                for at in range(total_coefs):
                    third_ref[at] = field[at]
                psi = lane_sum(third_ref[...].reshape(total_coefs * quarter, width), False)
                third_ref[...] = psi.reshape(total_coefs, quarter, width)
            elif part == 0:
                for at, (g, c) in enumerate(place):
                    h0_ref[g, c, i] = field[at] + (psi_ref[g, c] - third_ref[at])
            else:
                for at, (g, c) in enumerate(place):
                    psi = third_ref[at]
                    down = jnp.where(first_row, 0.0, pltpu.roll(psi, 1, 0))
                    h1_ref[g, c, i] = field[at] + (down - psi)
                    tail_ref[g, pl.ds(c * n + i, 1), :] = psi[quarter - 1 : quarter]
                    psi_ref[g, c] = psi
        return carry

    lax.fori_loop(0, n, one_plane, 0)
    for g, c in place:
        if kind == 0:
            pending_ref[g, c] = h0_ref[g, c, 0]
            last_psi_ref[g, c] = psi_ref[g, c]
        elif kind == 1:
            h0_ref[g, c, n] = psi_ref[g, c]
        else:
            h0_ref[g, c, n] = edge_h_ref[g, c] + psi_ref[g, c]
    step = chunk.nh + n
    for r in range(groups):
        g = partner(me, r, groups)
        for c in range(coefs):
            out_refs[r][c * step : c * step + chunk.nh] = h0_ref[g, c, chunk.h_from : chunk.h_from + chunk.nh]
            out_refs[r][c * step + chunk.nh : (c + 1) * step] = h1_ref[g, c]
        for t in range(tiles_for(coefs * n, quarter)):
            out_refs[r][coefs * step + t] = tail_ref[g, t * quarter : (t + 1) * quarter]


def sample_fields(chunk, me, messages, density, region, coefs, edges, after):
    groups = len(messages)
    _, quarter, width = messages[0].shape
    n = chunk.n
    f32 = jnp.float32
    shapes = [jax.ShapeDtypeStruct((chunk.back(coefs, quarter), quarter, width), f32)] * groups
    shapes.append(jax.ShapeDtypeStruct((n, quarter, width), f32))
    if chunk.kind == 0:
        shapes += [jax.ShapeDtypeStruct((2, groups, coefs, quarter, width), f32)] * 2
        shapes += [jax.ShapeDtypeStruct((groups, coefs, quarter, width), f32)] * 2
    operands = [me, *messages, density, region, *edges, *after]
    return pl.pallas_call(
        functools.partial(sample_kernel, chunk, groups, coefs, len(after)),
        in_specs=[SMEM] + [VMEM] * (len(operands) - 1 - len(after)) + [ANY] * len(after),
        out_specs=[VMEM] * len(shapes),
        out_shape=shapes,
        scratch_shapes=[
            pltpu.VMEM((2, groups, coefs, n, quarter, width), f32),
            pltpu.VMEM((2, groups, coefs, n + 1, quarter, width), f32),
            pltpu.VMEM((groups, tiles_for(2 * coefs * n, quarter) * quarter, width), f32),
            pltpu.VMEM((6, NT, quarter, width), f32),
            pltpu.VMEM((groups * coefs, quarter, width), f32),
            pltpu.VMEM((groups, coefs, quarter, width), f32),
            pltpu.VMEM((groups, coefs, n + 1, quarter, width), f32),
            pltpu.VMEM((groups, coefs, n, quarter, width), f32),
            pltpu.VMEM((groups, tiles_for(coefs * n, quarter) * quarter, width), f32),
        ],
        compiler_params=pltpu.CompilerParams(vmem_limit_bytes=SAMPLE_LIMIT),
        cost_estimate=LITTLE,
        name="samples%d" % chunk.kind,
    )(*operands)


def last_plane_kernel(chunk, coefs, me_ref, *refs):
    groups = len(refs) - 3
    message_refs, out_ref, row_ref = refs[:groups], refs[groups + 1], refs[groups + 2]
    quarter, width = message_refs[0].shape[1:]
    rows = quarter * groups
    step = chunk.nh + chunk.n
    me = me_ref[0]
    for c in range(coefs):
        for r in range(groups):
            here = pl.ds(pl.multiple_of(origin(me, r, groups) * quarter, quarter), quarter)
            row_ref[c, here] = message_refs[r][(c + 1) * step - 1]
            out_ref[c, 1, here] = message_refs[r][c * step + chunk.nh - 1]
        for r in range(groups):
            add_edge(row_ref.at[c], message_refs[r], chunk, coefs, c * chunk.n + chunk.n - 1, origin(me, r, groups) * quarter + quarter)
        out_ref[c, 0] = row_ref[c, 0:rows]


def add_edge(target, message_ref, chunk, coefs, spot, row):
    quarter = message_ref.shape[1]
    tile = coefs * (chunk.nh + chunk.n) + spot // quarter
    here = pl.ds(pl.multiple_of(row, quarter), 1)
    target[here] = target[here] + message_ref[tile, spot % quarter : spot % quarter + 1]


def last_plane(chunk, me, messages, coefs, after):
    groups = len(messages)
    _, quarter, width = messages[0].shape
    rows = groups * quarter
    return pl.pallas_call(
        functools.partial(last_plane_kernel, chunk, coefs),
        in_specs=[SMEM] + [VMEM] * groups + [ANY],
        out_specs=VMEM,
        out_shape=jax.ShapeDtypeStruct((coefs, 2, rows, width), jnp.float32),
        scratch_shapes=[pltpu.VMEM((coefs, rows + quarter, width), jnp.float32)],
        cost_estimate=LITTLE,
        name="last_plane",
    )(me, *messages, after)


def residual_kernel(chunks, groups, coefs, lo, hi, me_ref, *refs):
    message_refs = [refs[k * groups : (k + 1) * groups] for k in range(len(chunks))]
    refs = refs[len(chunks) * groups :]
    if lo == 0:
        halo_ref, objective_ref, _, out_ref, *refs = refs
    else:
        objective_ref, out_ref, *refs = refs
    h0_ref, h1_ref, taken, given, take_sems, give_sems = refs
    parts, planes, rows, width = objective_ref.shape[1:]
    quarter = rows // groups
    me = me_ref[0]
    row = lax.broadcasted_iota(jnp.int32, (rows, width), 0)
    lane = lax.broadcasted_iota(jnp.int32, (rows, width), 1)
    below = max(lo - 1, 0)
    wanted = pl.ds(lo, hi - lo)
    takes = [pltpu.make_async_copy(objective_ref.at[c, :, wanted], taken.at[c], take_sems.at[c]) for c in range(coefs)]
    gives = [pltpu.make_async_copy(given.at[c], out_ref.at[c, :, wanted], give_sems.at[c]) for c in range(coefs)]
    for copy in takes:
        copy.start()

    def lower_lane(v):
        return jnp.where(lane == 0, 0.0, pltpu.roll(v, 1, 1))

    for c in range(coefs):
        for chunk, messages in zip(chunks, message_refs):
            step = chunk.nh + chunk.n
            from_h0, to_h0 = max(chunk.lo + chunk.h_from, lo), min(chunk.lo + chunk.h_to, hi)
            from_h1, to_h1 = max(chunk.lo, below), min(chunk.hi, hi)
            for r in range(groups):
                here = pl.ds(pl.multiple_of(origin(me, r, groups) * quarter, quarter), quarter)
                if to_h0 > from_h0:
                    at = c * step - chunk.lo - chunk.h_from
                    h0_ref[c, from_h0 - below : to_h0 - below, here] = messages[r][at + from_h0 : at + to_h0]
                if to_h1 > from_h1:
                    at = c * step + chunk.nh - chunk.lo
                    h1_ref[c, from_h1 - below : to_h1 - below, here] = messages[r][at + from_h1 : at + to_h1]
            for r in range(groups):
                above = origin(me, r, groups) * quarter + quarter
                for i in range(from_h1, to_h1):
                    add_edge(h1_ref.at[c, i - below], messages[r], chunk, coefs, c * chunk.n + i - chunk.lo, above)
    for c in range(coefs):
        takes[c].wait()
        before = halo_ref[c, 0] if lo == 0 else h1_ref[c, 0, 0:rows]
        for i in range(lo, hi):
            h0 = h0_ref[c, i - below]
            if i == 0:
                h0 = h0 + halo_ref[c, 1]
            h1 = h1_ref[c, i - below, 0:rows]
            given[c, 0, i - lo] = taken[c, 0, i - lo] - (2.0 / NT) * (lower_lane(h1) - h1)
            given[c, 1, i - lo] = taken[c, 1, i - lo] - (2.0 / NT) * (h0 - lower_lane(h0))
            lower_row = jnp.where(row == 0, 0.0, pltpu.roll(h0, 1, 0))
            given[c, 2, i - lo] = taken[c, 2, i - lo] - (2.0 / NT) * ((lower_row - h0) - (before - h1))
            before = h1
        gives[c].start()
    for copy in gives:
        copy.wait()


def residual(chunks, me, returned, objective_hat, lo, hi, halo=None, begun=None):
    coefs, parts, planes, rows, width = objective_hat.shape
    groups = len(returned[0])
    quarter = rows // groups
    held = hi - max(lo - 1, 0)
    operands = [me] + [m for messages in returned for m in messages]
    specs = [SMEM] + [VMEM] * (len(operands) - 1)
    if lo == 0:
        operands.append(halo)
        specs.append(VMEM)
    operands.append(objective_hat)
    specs.append(HBM)
    aliases = {}
    if lo == 0:
        aliases = {len(operands): 0}
        operands.append(begun)
        specs.append(HBM)
    return pl.pallas_call(
        functools.partial(residual_kernel, chunks, groups, coefs, lo, hi),
        in_specs=specs,
        out_specs=HBM,
        out_shape=jax.ShapeDtypeStruct(objective_hat.shape, jnp.float32),
        input_output_aliases=aliases,
        scratch_shapes=[
            pltpu.VMEM((coefs, held, rows, width), jnp.float32),
            pltpu.VMEM((coefs, held, rows + quarter, width), jnp.float32),
            pltpu.VMEM((coefs, parts, hi - lo, rows, width), jnp.float32),
            pltpu.VMEM((coefs, parts, hi - lo, rows, width), jnp.float32),
            pltpu.SemaphoreType.DMA((coefs,)),
            pltpu.SemaphoreType.DMA((coefs,)),
        ],
        compiler_params=pltpu.CompilerParams(vmem_limit_bytes=RESIDUAL_LIMIT),
        cost_estimate=LITTLE,
        name="residual_first" if lo == 0 else "residual_rest",
    )(*operands)


def local(state_hat, adjoint_hat, objective_hat, density, region):
    groups = lax.axis_size("sample")
    coefs, parts, planes, rows, width = state_hat.shape
    me = lax.axis_index("sample").astype(jnp.int32).reshape(1)
    first = planes // 4
    last = planes - first
    middle_chunk, last_chunk = Chunk(0, first, last), Chunk(1, last, planes)
    first_chunk = Chunk(2, 0, first, last_chunk.sent(coefs, rows // groups))
    *sent0, first_planes = gauge((middle_chunk,), groups, me, state_hat, adjoint_hat)
    cells0 = exchange(sent0)
    upper = passed_along(first_planes, "space", -1)
    sent1 = gauge((last_chunk, first_chunk), groups, me, state_hat, adjoint_hat, upper)
    cells1 = exchange(sent1)
    *out0, grad0, first_q, last_q, pending, last_psi = sample_fields(middle_chunk, me, cells0, density, region, coefs, (), sent1[:1])
    back0 = exchange(out0)
    *out1, grad1 = sample_fields(last_chunk, me, cells1, density, region, coefs, (last_q, last_psi), ())
    back1 = exchange(out1)
    *out2, grad2 = sample_fields(first_chunk, me, cells1, density, region, coefs, (first_q, pending), out1[:1])
    back2 = exchange(out2)
    lower = passed_along(last_plane(last_chunk, me, back1, coefs, out2[0]), "space", 1)
    begun = residual((middle_chunk, last_chunk), me, (back0, back1), objective_hat, first + 1, planes)
    adjoint_residual = residual((middle_chunk, first_chunk), me, (back0, back2), objective_hat, 0, first + 1, lower, begun)
    return adjoint_residual, jnp.concatenate([grad2, grad0, grad1], axis=0)


def solution(mesh):
    in_specs = (
        P("sample", None, "space", None, None),
        P("sample", None, "space", None, None),
        P("sample", None, "space", None, None),
        P("space", None, None),
        P("space", None, None),
    )
    out_specs = (P("sample", None, "space", None, None), P("space", "sample", None))
    return jax.shard_map(local, mesh=mesh, in_specs=in_specs, out_specs=out_specs, check_vma=False)
```

```python
import functools
import math

import jax
import jax.numpy as jnp
from jax import lax
from jax.experimental import pallas as pl
from jax.experimental.pallas import tpu as pltpu
from jax.sharding import PartitionSpec as P

NT = 40
magnet_reluct = 0.95
iron_floor = 0.05
saturation = 1.0
GAUGE_LIMIT = 16 * 1024 * 1024
FIRST_LIMIT = 62 * 1024 * 1024
SAMPLE_LIMIT = 16 * 1024 * 1024
RESIDUAL_LIMIT = 16 * 1024 * 1024
LAST_LIMIT = 4 * 1024 * 1024


def passed_along(array, axis, by):
    size = lax.axis_size(axis)
    pairs = [(i, i + by) for i in range(size) if 0 <= i + by < size]
    return lax.ppermute(array, axis, pairs)


def angle(n, m, period):
    return 2.0 * math.pi * ((n * m) % period) / period


def weighted(terms):
    total = None
    for factor, value in terms:
        if abs(factor) < 1e-12:
            continue
        if abs(factor - 1.0) < 1e-12:
            total = value if total is None else total + value
        elif abs(factor + 1.0) < 1e-12:
            total = -value if total is None else total - value
        else:
            total = factor * value if total is None else total + factor * value
    return total


def add(a, b):
    return b if a is None else (a if b is None else a + b)


def sub(a, b):
    return a if b is None else (-b if a is None else a - b)


def synth(cos_of, sin_of, period):
    if period % 2:
        cos_part = {n: weighted([(math.cos(angle(n, m, period)), v) for m, v in cos_of.items()]) for n in range((period + 1) // 2)}
        sin_part = {n: weighted([(math.sin(angle(n, m, period)), v) for m, v in sin_of.items()]) for n in range((period + 1) // 2)}
        x = [None] * period
        for n in range((period + 1) // 2):
            x[n] = add(cos_part[n], sin_part[n])
            if n:
                x[period - n] = sub(cos_part[n], sin_part[n])
        return x
    half = period // 2
    odd = [None] * half
    cos_odd = {m: v for m, v in cos_of.items() if m % 2}
    sin_odd = {m: v for m, v in sin_of.items() if m % 2}
    for n in range(half // 2 + 1):
        c = weighted([(math.cos(angle(n, m, period)), v) for m, v in cos_odd.items()])
        s = weighted([(math.sin(angle(n, m, period)), v) for m, v in sin_odd.items()])
        odd[n] = add(c, s)
        if n and half - n != n:
            odd[half - n] = sub(s, c)
    cos_even = {m // 2: v for m, v in cos_of.items() if m % 2 == 0}
    sin_even = {m // 2: v for m, v in sin_of.items() if m % 2 == 0}
    if not cos_even:
        return [odd[n] for n in range(half)] + [sub(None, odd[n]) for n in range(half)]
    even = synth(cos_even, sin_even, half)
    return [add(even[n], odd[n]) for n in range(half)] + [sub(even[n], odd[n]) for n in range(half)]


def analyse(x, orders, period):
    if period % 2:
        plus = {n: (x[n] + x[period - n] if n else x[0]) for n in range((period + 1) // 2)}
        minus = {n: x[n] - x[period - n] for n in range(1, (period + 1) // 2)}
        cos_of = {m: weighted([(math.cos(angle(n, m, period)), v) for n, v in plus.items()]) for m in orders}
        sin_of = {m: weighted([(math.sin(angle(n, m, period)), v) for n, v in minus.items()]) for m in orders}
        return cos_of, sin_of
    half = period // 2
    odd = [x[n] - x[n + half] for n in range(half)]
    cos_in, sin_in = {}, {}
    for n in range(half // 2 + 1):
        if n and half - n != n:
            cos_in[n] = odd[n] - odd[half - n]
            sin_in[n] = odd[n] + odd[half - n]
        else:
            cos_in[n] = odd[n]
            sin_in[n] = odd[n]
    cos_of = {m: weighted([(math.cos(angle(n, m, period)), v) for n, v in cos_in.items()]) for m in orders if m % 2}
    sin_of = {m: weighted([(math.sin(angle(n, m, period)), v) for n, v in sin_in.items()]) for m in orders if m % 2}
    lower = [m // 2 for m in orders if m % 2 == 0]
    if lower:
        even = [x[n] + x[n + half] for n in range(half)]
        cos_even, sin_even = analyse(even, lower, half)
        cos_of.update({2 * m: v for m, v in cos_even.items()})
        sin_of.update({2 * m: v for m, v in sin_even.items()})
    return cos_of, sin_of


def lane_sum(rows, upward):
    width = rows.shape[1]
    source = lax.broadcasted_iota(jnp.int32, (2 * width, width), 0)
    source = jnp.where(source >= width, source - width, source)
    target = lax.broadcasted_iota(jnp.int32, (2 * width, width), 1)
    chosen = source >= target if upward else source <= target
    ones = jnp.where(chosen, 1.0, 0.0).astype(jnp.bfloat16)
    high = rows.astype(jnp.bfloat16)
    low = (rows - high.astype(jnp.float32)).astype(jnp.bfloat16)
    return jnp.dot(jnp.concatenate([high, low], axis=1), ones, preferred_element_type=jnp.float32)


def partner(me, r, groups):
    if groups & (groups - 1) == 0:
        return jnp.bitwise_xor(me, r)
    return lax.rem(me + r, groups)


def origin(me, r, groups):
    if groups & (groups - 1) == 0:
        return jnp.bitwise_xor(me, r)
    return lax.rem(me + groups - r, groups)


def exchange(messages):
    groups = len(messages)
    taken = [messages[0]] + [None] * (groups - 1)
    for r in list(range(2, groups)) + [1]:
        if groups & (groups - 1) == 0:
            pairs = [(i, i ^ r) for i in range(groups)]
        else:
            pairs = [(i, (i + r) % groups) for i in range(groups)]
        taken[r] = lax.ppermute(messages[r], "sample", pairs)
    return taken


def tiles_for(rows, quarter):
    return -(-rows // quarter)


VMEM = pl.BlockSpec(memory_space=pltpu.VMEM)
SMEM = pl.BlockSpec(memory_space=pltpu.SMEM)
HBM = pl.BlockSpec(memory_space=pltpu.HBM)
ANY = pl.BlockSpec(memory_space=pl.ANY)
MUCH = pl.CostEstimate(flops=10**6, bytes_accessed=6 * 10**7, transcendentals=0)
LITTLE = pl.CostEstimate(flops=1000, bytes_accessed=1000, transcendentals=0)


class Chunk:
    def __init__(self, kind, lo, hi, at=0):
        self.at = at
        self.kind, self.lo, self.hi, self.n = kind, lo, hi, hi - lo
        self.q_from = 1 if kind == 1 else 0
        self.q_to = self.n if kind == 2 else self.n + 1
        self.nq = self.q_to - self.q_from
        self.h_from = 1 if kind == 0 else 0
        self.h_to = self.n + 1 if kind == 2 else self.n
        self.nh = self.h_to - self.h_from + (1 if kind == 1 else 0)

    def sent(self, coefs, quarter):
        return 2 * coefs * (self.n + self.nq) + tiles_for(2 * coefs * self.n, quarter)

    def back(self, coefs, quarter):
        return coefs * (self.nh + self.n) + tiles_for(coefs * self.n, quarter)


def gauge_kernel(chunks, groups, has_halo, me_ref, state_ref, adjoint_ref, *rest):
    if has_halo:
        halo_ref, rest = rest[0], rest[1:]
    out_refs, rest = rest[:groups], rest[groups:]
    if not has_halo:
        first_ref, first_sems = rest[0], rest[-1]
        rest = rest[1:-1]
    coefs, parts, planes, rows, width = state_ref.shape
    quarter = rows // groups
    me = me_ref[0]
    sources = (state_ref, adjoint_ref)
    copies = {}
    for which in range(2):
        for at, chunk in enumerate(chunks):
            held, sems = rest[5 * at], rest[5 * at + 4]
            planes_here = pl.ds(chunk.lo, held.shape[3])
            for c in range(coefs):
                copy = pltpu.make_async_copy(sources[which].at[c, :, planes_here], held.at[which, c], sems.at[which, c])
                copy.start()
                copies[which, at, c] = copy
    firsts = []
    if not has_halo:
        for which in range(2):
            for c in range(coefs):
                source = sources[which].at[c, pl.ds(1, 2), 0]
                firsts.append(pltpu.make_async_copy(source, first_ref.at[which, c], first_sems.at[which, c]))
                firsts[-1].start()
    for which in range(2):
        for at, chunk in enumerate(chunks):
            held, phi_held, p_held, q_held, _ = rest[5 * at : 5 * at + 5]
            n, nq = chunk.n, chunk.nq
            own = held.shape[3]
            last_row = lax.broadcasted_iota(jnp.int32, (n + 1, rows, width), 1) == rows - 1
            zero_rows = jnp.zeros((n, quarter, width), jnp.float32)
            for c in range(coefs):
                copies[which, at, c].wait()
            third = held[which, :, 2]
            if own == n:
                third = jnp.concatenate([third, halo_ref[which, :, 1][:, None]], axis=1)
            phi_all = lane_sum(third.reshape(coefs * (n + 1) * rows, width), True)
            phi_held[...] = phi_all.reshape(coefs, n + 1, rows, width)
            for c in range(coefs):
                second = held[which, c, 1]
                if own == n:
                    second = jnp.concatenate([second, halo_ref[which, c, 0][None]], axis=0)
                phi = phi_held[c]
                phi_up = jnp.where(last_row, 0.0, pltpu.roll(phi, rows - 1, 1))
                p_held[which, c, :, 0:rows] = held[which, c, 0, 0:n] + phi[1:] - phi[:-1]
                p_held[which, c, :, rows : rows + quarter] = zero_rows
                q_held[which, c] = (second + (phi_up - phi))[chunk.q_from : chunk.q_to]
            for c in range(coefs):
                base = chunk.at + (which * coefs + c) * (n + nq)
                for r in range(groups):
                    start = pl.multiple_of(partner(me, r, groups) * quarter, quarter)
                    out_refs[r][base : base + n] = p_held[which, c, :, pl.ds(start, quarter)]
                    out_refs[r][base + n : base + n + nq] = q_held[which, c, :, pl.ds(start, quarter)]
                    for i in range(n):
                        spot = (which * coefs + c) * n + i
                        edge = p_held[which, c, i, pl.ds(pl.multiple_of(start + quarter, quarter), quarter)]
                        tile = chunk.at + 2 * coefs * (n + nq) + spot // quarter
                        out_refs[r][tile, spot % quarter : spot % quarter + 1] = edge[0:1]
    for copy in firsts:
        copy.wait()


def gauge(chunks, groups, me, state_hat, adjoint_hat, halo=None):
    coefs, parts, planes, rows, width = state_hat.shape
    quarter = rows // groups
    tiles = sum(chunk.sent(coefs, quarter) for chunk in chunks)
    shapes = [jax.ShapeDtypeStruct((tiles, quarter, width), jnp.float32)] * groups
    scratch = []
    for chunk in chunks:
        own = min(chunk.n + 1, planes - chunk.lo)
        scratch += [
            pltpu.VMEM((2, coefs, parts, own, rows, width), jnp.float32),
            pltpu.VMEM((coefs, chunk.n + 1, rows, width), jnp.float32),
            pltpu.VMEM((2, coefs, chunk.n, rows + quarter, width), jnp.float32),
            pltpu.VMEM((2, coefs, chunk.nq, rows, width), jnp.float32),
            pltpu.SemaphoreType.DMA((2, coefs)),
        ]
    operands, specs = [me, state_hat, adjoint_hat], [SMEM, HBM, HBM]
    if halo is None:
        shapes.append(jax.ShapeDtypeStruct((2, coefs, 2, rows, width), jnp.float32))
        scratch.append(pltpu.SemaphoreType.DMA((2, coefs)))
    else:
        operands.append(halo)
        specs.append(VMEM)
    return pl.pallas_call(
        functools.partial(gauge_kernel, chunks, groups, halo is not None),
        in_specs=specs,
        out_specs=[VMEM] * len(shapes),
        out_shape=shapes,
        scratch_shapes=scratch,
        compiler_params=pltpu.CompilerParams(vmem_limit_bytes=FIRST_LIMIT if halo is None else GAUGE_LIMIT),
        cost_estimate=LITTLE,
        name="gauge_middle" if halo is None else "gauge_ends",
    )(*operands)


def sample_kernel(chunk, groups, coefs, later, *refs):
    n, nq, kind = chunk.n, chunk.nq, chunk.kind
    me_ref, message_refs, refs = refs[0], refs[1 : 1 + groups], refs[1 + groups :]
    density_ref, region_ref, refs = refs[0], refs[1], refs[2:]
    edge_q_ref = edge_h_ref = None
    if kind:
        edge_q_ref, edge_h_ref, refs = refs[0], refs[1], refs[2:]
    carried_refs = ()
    if kind == 2:
        carried_refs, refs = refs[: groups - 1], refs[groups - 1 :]
    refs = refs[later:]
    out_refs, grad_ref, refs = refs[:groups], refs[groups], refs[groups + 1 :]
    if kind == 0:
        first_q_ref, last_q_ref, pending_ref, last_psi_ref = refs[:4]
        refs = refs[4:]
    p_ref, q_ref, edge_ref, time_ref, third_ref, psi_ref, h0_ref, h1_ref, tail_ref = refs
    quarter, width = p_ref.shape[4:]
    shape = (quarter, width)
    me = me_ref[0]
    row = lax.broadcasted_iota(jnp.int32, shape, 0)
    lane = lax.broadcasted_iota(jnp.int32, shape, 1)
    last_lane = lane == width - 1
    last_row = row == quarter - 1
    first_row = row == 0
    my_rows = pl.ds(pl.multiple_of(me * quarter, quarter), quarter)
    total_coefs = groups * coefs
    orders = list(range(1, total_coefs // 2 + 1))
    place = [(c // coefs, c % coefs) for c in range(total_coefs)]

    for r in range(groups):
        g = origin(me, r, groups)
        for which in range(2):
            for c in range(coefs):
                base = chunk.at + (which * coefs + c) * (n + nq)
                p_ref[which, g, c] = message_refs[r][base : base + n]
                q_ref[which, g, c, chunk.q_from : chunk.q_to] = message_refs[r][base + n : base + n + nq]
        for t in range(tiles_for(2 * coefs * n, quarter)):
            edge_ref[g, t * quarter : (t + 1) * quarter] = message_refs[r][chunk.at + 2 * coefs * (n + nq) + t]
    for which in range(2):
        for g in range(groups):
            for c in range(coefs):
                if kind == 0:
                    first_q_ref[which, g, c] = q_ref[which, g, c, 0]
                    last_q_ref[which, g, c] = q_ref[which, g, c, n]
                elif kind == 1:
                    q_ref[which, g, c, 0] = edge_q_ref[which, g, c]
                else:
                    q_ref[which, g, c, n] = edge_q_ref[which, g, c]
    if kind == 1:
        psi_ref[...] = edge_h_ref[...]
    else:
        psi_ref[...] = jnp.zeros(psi_ref.shape, jnp.float32)

    def next_lane(v):
        return jnp.where(last_lane, 0.0, pltpu.roll(v, width - 1, 1))

    def one_plane(i, carry):
        for which in range(2):
            for part in range(3):
                flux = []
                for g, c in place:
                    if part == 0:
                        q = q_ref[which, g, c, i]
                        flux.append(q - next_lane(q))
                    elif part == 1:
                        p = p_ref[which, g, c, i]
                        flux.append(next_lane(p) - p)
                    else:
                        p = p_ref[which, g, c, i]
                        edge = edge_ref[g, pl.ds((which * coefs + c) * n + i, 1), :]
                        up = jnp.where(last_row, jnp.broadcast_to(edge, shape), pltpu.roll(p, quarter - 1, 0))
                        flux.append(q_ref[which, g, c, i + 1] - q_ref[which, g, c, i] - (up - p))
                samples = synth({m: flux[2 * m - 2] for m in orders}, {m: flux[2 * m - 1] for m in orders}, NT)
                for k in range(NT):
                    time_ref[which * 3 + part, k] = samples[k]
        density = density_ref[chunk.lo + i, my_rows]
        region = region_ref[chunk.lo + i, my_rows]
        iron = region == 0
        share = jnp.where(iron, density * density * density, 0.0) * (1.0 - iron_floor)
        slope = jnp.where(iron, 3.0 * density * density, 0.0)
        base = jnp.where(region == 1, magnet_reluct, 1.0)
        total = jnp.zeros(shape, jnp.float32)
        for k in range(NT):
            b = [time_ref[j, k] for j in range(3)]
            a = [time_ref[3 + j, k] for j in range(3)]
            square = b[0] * b[0] + b[1] * b[1] + b[2] * b[2]
            inner = b[0] * a[0] + b[1] * a[1] + b[2] * a[2]
            inverse = 1.0 / (square + saturation)
            scaled = share * inverse
            reluct_now = base - scaled
            ratio = inverse * inner
            total = total + ratio
            along = scaled * ratio
            along = along + along
            for j in range(3):
                time_ref[j, k] = reluct_now * a[j] + along * b[j]
        grad_ref[i] = ((1.0 - iron_floor) / NT) * slope * total
        for part in (2, 0, 1):
            cos_of, sin_of = analyse([time_ref[part, k] for k in range(NT)], orders, NT)
            field = []
            for m in orders:
                field += [cos_of[m], sin_of[m]]
            if part == 2:
                for at in range(total_coefs):
                    third_ref[at] = field[at]
                psi = lane_sum(third_ref[...].reshape(total_coefs * quarter, width), False)
                third_ref[...] = psi.reshape(total_coefs, quarter, width)
            elif part == 0:
                for at, (g, c) in enumerate(place):
                    h0_ref[g, c, i] = field[at] + (psi_ref[g, c] - third_ref[at])
            else:
                for at, (g, c) in enumerate(place):
                    psi = third_ref[at]
                    down = jnp.where(first_row, 0.0, pltpu.roll(psi, 1, 0))
                    h1_ref[g, c, i] = field[at] + (down - psi)
                    tail_ref[g, pl.ds(c * n + i, 1), :] = psi[quarter - 1 : quarter]
                    psi_ref[g, c] = psi
        return carry

    lax.fori_loop(0, n, one_plane, 0)
    for g, c in place:
        if kind == 0:
            pending_ref[g, c] = h0_ref[g, c, 0]
            last_psi_ref[g, c] = psi_ref[g, c]
        elif kind == 1:
            h0_ref[g, c, n] = psi_ref[g, c]
        else:
            h0_ref[g, c, n] = edge_h_ref[g, c] + psi_ref[g, c]
    step = chunk.nh + n
    for r in range(groups):
        g = partner(me, r, groups)
        for c in range(coefs):
            out_refs[r][c * step : c * step + chunk.nh] = h0_ref[g, c, chunk.h_from : chunk.h_from + chunk.nh]
            out_refs[r][c * step + chunk.nh : (c + 1) * step] = h1_ref[g, c]
        for t in range(tiles_for(coefs * n, quarter)):
            out_refs[r][coefs * step + t] = tail_ref[g, t * quarter : (t + 1) * quarter]
    for r, carried_ref in enumerate(carried_refs, 1):
        out_refs[r][chunk.back(coefs, quarter) :] = carried_ref[...]


def sample_fields(chunk, me, messages, density, region, coefs, edges, after):
    groups = len(messages)
    _, quarter, width = messages[0].shape
    n = chunk.n
    f32 = jnp.float32
    shapes = [jax.ShapeDtypeStruct((chunk.back(coefs, quarter), quarter, width), f32)] * groups
    if chunk.kind == 2:
        both = chunk.back(coefs, quarter) + edges[2].shape[0]
        shapes[1:] = [jax.ShapeDtypeStruct((both, quarter, width), f32)] * (groups - 1)
    shapes.append(jax.ShapeDtypeStruct((n, quarter, width), f32))
    if chunk.kind == 0:
        shapes += [jax.ShapeDtypeStruct((2, groups, coefs, quarter, width), f32)] * 2
        shapes += [jax.ShapeDtypeStruct((groups, coefs, quarter, width), f32)] * 2
    operands = [me, *messages, density, region, *edges, *after]
    return pl.pallas_call(
        functools.partial(sample_kernel, chunk, groups, coefs, len(after)),
        in_specs=[SMEM] + [VMEM] * (len(operands) - 1 - len(after)) + [ANY] * len(after),
        out_specs=[VMEM] * len(shapes),
        out_shape=shapes,
        scratch_shapes=[
            pltpu.VMEM((2, groups, coefs, n, quarter, width), f32),
            pltpu.VMEM((2, groups, coefs, n + 1, quarter, width), f32),
            pltpu.VMEM((groups, tiles_for(2 * coefs * n, quarter) * quarter, width), f32),
            pltpu.VMEM((6, NT, quarter, width), f32),
            pltpu.VMEM((groups * coefs, quarter, width), f32),
            pltpu.VMEM((groups, coefs, quarter, width), f32),
            pltpu.VMEM((groups, coefs, n + 1, quarter, width), f32),
            pltpu.VMEM((groups, coefs, n, quarter, width), f32),
            pltpu.VMEM((groups, tiles_for(coefs * n, quarter) * quarter, width), f32),
        ],
        compiler_params=pltpu.CompilerParams(vmem_limit_bytes=SAMPLE_LIMIT),
        cost_estimate=LITTLE,
        name="samples%d" % chunk.kind,
    )(*operands)


def last_plane_kernel(chunk, coefs, me_ref, *refs):
    groups = len(refs) - 3
    message_refs, out_ref, row_ref = refs[:groups], refs[groups + 1], refs[groups + 2]
    quarter, width = message_refs[0].shape[1:]
    rows = quarter * groups
    step = chunk.nh + chunk.n
    me = me_ref[0]
    for c in range(coefs):
        for r in range(groups):
            here = pl.ds(pl.multiple_of(origin(me, r, groups) * quarter, quarter), quarter)
            row_ref[c, here] = message_refs[r][(c + 1) * step - 1]
            out_ref[c, 1, here] = message_refs[r][c * step + chunk.nh - 1]
        for r in range(groups):
            add_edge(row_ref.at[c], message_refs[r], chunk, coefs, c * chunk.n + chunk.n - 1, origin(me, r, groups) * quarter + quarter)
        out_ref[c, 0] = row_ref[c, 0:rows]


def add_edge(target, message_ref, chunk, coefs, spot, row, shift=0):
    quarter = message_ref.shape[1]
    tile = shift + coefs * (chunk.nh + chunk.n) + spot // quarter
    here = pl.ds(pl.multiple_of(row, quarter), 1)
    target[here] = target[here] + message_ref[tile, spot % quarter : spot % quarter + 1]


def last_plane(chunk, me, messages, coefs, after):
    groups = len(messages)
    _, quarter, width = messages[0].shape
    rows = groups * quarter
    return pl.pallas_call(
        functools.partial(last_plane_kernel, chunk, coefs),
        in_specs=[SMEM] + [VMEM] * groups + [ANY],
        out_specs=VMEM,
        out_shape=jax.ShapeDtypeStruct((coefs, 2, rows, width), jnp.float32),
        scratch_shapes=[pltpu.VMEM((coefs, rows + quarter, width), jnp.float32)],
        compiler_params=pltpu.CompilerParams(vmem_limit_bytes=LAST_LIMIT),
        cost_estimate=LITTLE,
        name="last_plane",
    )(me, *messages, after)


def residual_kernel(chunks, shifts, groups, coefs, lo, hi, me_ref, *refs):
    message_refs = [refs[k * groups : (k + 1) * groups] for k in range(len(chunks))]
    refs = refs[len(chunks) * groups :]
    if lo == 0:
        halo_ref, objective_ref, _, out_ref, *refs = refs
    else:
        objective_ref, out_ref, *refs = refs
    h0_ref, h1_ref, taken, given, take_sems, give_sems = refs
    parts, planes, rows, width = objective_ref.shape[1:]
    quarter = rows // groups
    me = me_ref[0]
    row = lax.broadcasted_iota(jnp.int32, (rows, width), 0)
    lane = lax.broadcasted_iota(jnp.int32, (rows, width), 1)
    below = max(lo - 1, 0)
    wanted = pl.ds(lo, hi - lo)
    takes = [pltpu.make_async_copy(objective_ref.at[c, :, wanted], taken.at[c], take_sems.at[c]) for c in range(coefs)]
    gives = [pltpu.make_async_copy(given.at[c], out_ref.at[c, :, wanted], give_sems.at[c]) for c in range(coefs)]
    for copy in takes:
        copy.start()

    def lower_lane(v):
        return jnp.where(lane == 0, 0.0, pltpu.roll(v, 1, 1))

    for c in range(coefs):
        for chunk, shift, messages in zip(chunks, shifts, message_refs):
            step = chunk.nh + chunk.n
            from_h0, to_h0 = max(chunk.lo + chunk.h_from, lo), min(chunk.lo + chunk.h_to, hi)
            from_h1, to_h1 = max(chunk.lo, below), min(chunk.hi, hi)
            for r in range(groups):
                here = pl.ds(pl.multiple_of(origin(me, r, groups) * quarter, quarter), quarter)
                if to_h0 > from_h0:
                    at = shift[r] + c * step - chunk.lo - chunk.h_from
                    h0_ref[c, from_h0 - below : to_h0 - below, here] = messages[r][at + from_h0 : at + to_h0]
                if to_h1 > from_h1:
                    at = shift[r] + c * step + chunk.nh - chunk.lo
                    h1_ref[c, from_h1 - below : to_h1 - below, here] = messages[r][at + from_h1 : at + to_h1]
            for r in range(groups):
                above = origin(me, r, groups) * quarter + quarter
                for i in range(from_h1, to_h1):
                    add_edge(h1_ref.at[c, i - below], messages[r], chunk, coefs, c * chunk.n + i - chunk.lo, above, shift[r])
    for c in range(coefs):
        takes[c].wait()
        before = halo_ref[c, 0] if lo == 0 else h1_ref[c, 0, 0:rows]
        for i in range(lo, hi):
            h0 = h0_ref[c, i - below]
            if i == 0:
                h0 = h0 + halo_ref[c, 1]
            h1 = h1_ref[c, i - below, 0:rows]
            given[c, 0, i - lo] = taken[c, 0, i - lo] - (2.0 / NT) * (lower_lane(h1) - h1)
            given[c, 1, i - lo] = taken[c, 1, i - lo] - (2.0 / NT) * (h0 - lower_lane(h0))
            lower_row = jnp.where(row == 0, 0.0, pltpu.roll(h0, 1, 0))
            given[c, 2, i - lo] = taken[c, 2, i - lo] - (2.0 / NT) * ((lower_row - h0) - (before - h1))
            before = h1
        gives[c].start()
    for copy in gives:
        copy.wait()


def residual(chunks, shifts, me, returned, objective_hat, lo, hi, halo=None, begun=None):
    coefs, parts, planes, rows, width = objective_hat.shape
    groups = len(returned[0])
    quarter = rows // groups
    held = hi - max(lo - 1, 0)
    operands = [me] + [m for messages in returned for m in messages]
    specs = [SMEM] + [VMEM] * (len(operands) - 1)
    if lo == 0:
        operands.append(halo)
        specs.append(VMEM)
    operands.append(objective_hat)
    specs.append(HBM)
    aliases = {}
    if lo == 0:
        aliases = {len(operands): 0}
        operands.append(begun)
        specs.append(HBM)
    return pl.pallas_call(
        functools.partial(residual_kernel, chunks, shifts, groups, coefs, lo, hi),
        in_specs=specs,
        out_specs=HBM,
        out_shape=jax.ShapeDtypeStruct(objective_hat.shape, jnp.float32),
        input_output_aliases=aliases,
        scratch_shapes=[
            pltpu.VMEM((coefs, held, rows, width), jnp.float32),
            pltpu.VMEM((coefs, held, rows + quarter, width), jnp.float32),
            pltpu.VMEM((coefs, parts, hi - lo, rows, width), jnp.float32),
            pltpu.VMEM((coefs, parts, hi - lo, rows, width), jnp.float32),
            pltpu.SemaphoreType.DMA((coefs,)),
            pltpu.SemaphoreType.DMA((coefs,)),
        ],
        compiler_params=pltpu.CompilerParams(vmem_limit_bytes=RESIDUAL_LIMIT),
        cost_estimate=LITTLE if lo == 0 else MUCH,
        name="residual_first" if lo == 0 else "residual_rest",
    )(*operands)


def local(state_hat, adjoint_hat, objective_hat, density, region):
    groups = lax.axis_size("sample")
    coefs, parts, planes, rows, width = state_hat.shape
    me = lax.axis_index("sample").astype(jnp.int32).reshape(1)
    first = planes // 4
    last = planes - first
    middle_chunk, last_chunk = Chunk(0, first, last), Chunk(1, last, planes)
    first_chunk = Chunk(2, 0, first, last_chunk.sent(coefs, rows // groups))
    *sent0, first_planes = gauge((middle_chunk,), groups, me, state_hat, adjoint_hat)
    cells0 = exchange(sent0)
    upper = passed_along(first_planes, "space", -1)
    sent1 = gauge((last_chunk, first_chunk), groups, me, state_hat, adjoint_hat, upper)
    cells1 = exchange(sent1)
    *out0, grad0, first_q, last_q, pending, last_psi = sample_fields(middle_chunk, me, cells0, density, region, coefs, (), sent1[:1])
    *out1, grad1 = sample_fields(last_chunk, me, cells1, density, region, coefs, (last_q, last_psi), ())
    back1 = exchange(out1)
    *out2, grad2 = sample_fields(first_chunk, me, cells1, density, region, coefs, (first_q, pending, *out0[1:]), out1[:1])
    back2 = exchange(out2)
    back0 = [out0[0], *back2[1:]]
    none = [0] * groups
    carried = [0] + [first_chunk.back(coefs, rows // groups)] * (groups - 1)
    lower = passed_along(last_plane(last_chunk, me, back1, coefs, out2[0]), "space", 1)
    chunks = (middle_chunk, last_chunk, first_chunk)
    begun = residual(chunks, (carried, none, none), me, (back0, back1, back2), objective_hat, 1, planes)
    adjoint_residual = residual((first_chunk,), (none,), me, (back2,), objective_hat, 0, 1, lower, begun)
    return adjoint_residual, jnp.concatenate([grad2, grad0, grad1], axis=0)


def solution(mesh):
    in_specs = (
        P("sample", None, "space", None, None),
        P("sample", None, "space", None, None),
        P("sample", None, "space", None, None),
        P("space", None, None),
        P("space", None, None),
    )
    out_specs = (P("sample", None, "space", None, None), P("space", "sample", None))
    return jax.shard_map(local, mesh=mesh, in_specs=in_specs, out_specs=out_specs, check_vma=False)
```

```python
import functools
import math

import jax
import jax.numpy as jnp
from jax import lax
from jax.experimental import pallas as pl
from jax.experimental.pallas import tpu as pltpu
from jax.sharding import PartitionSpec as P

NT = 40
magnet_reluct = 0.95
iron_floor = 0.05
saturation = 1.0
GAUGE_LIMIT = 16 * 1024 * 1024
FIRST_LIMIT = 62 * 1024 * 1024
SAMPLE_LIMIT = 16 * 1024 * 1024
RESIDUAL_LIMIT = 16 * 1024 * 1024
LAST_LIMIT = 4 * 1024 * 1024


def passed_along(array, axis, by):
    size = lax.axis_size(axis)
    pairs = [(i, i + by) for i in range(size) if 0 <= i + by < size]
    return lax.ppermute(array, axis, pairs)


def angle(n, m, period):
    return 2.0 * math.pi * ((n * m) % period) / period


def weighted(terms):
    total = None
    for factor, value in terms:
        if abs(factor) < 1e-12:
            continue
        if abs(factor - 1.0) < 1e-12:
            total = value if total is None else total + value
        elif abs(factor + 1.0) < 1e-12:
            total = -value if total is None else total - value
        else:
            total = factor * value if total is None else total + factor * value
    return total


def add(a, b):
    return b if a is None else (a if b is None else a + b)


def sub(a, b):
    return a if b is None else (-b if a is None else a - b)


def synth(cos_of, sin_of, period):
    if period % 2:
        cos_part = {n: weighted([(math.cos(angle(n, m, period)), v) for m, v in cos_of.items()]) for n in range((period + 1) // 2)}
        sin_part = {n: weighted([(math.sin(angle(n, m, period)), v) for m, v in sin_of.items()]) for n in range((period + 1) // 2)}
        x = [None] * period
        for n in range((period + 1) // 2):
            x[n] = add(cos_part[n], sin_part[n])
            if n:
                x[period - n] = sub(cos_part[n], sin_part[n])
        return x
    half = period // 2
    odd = [None] * half
    cos_odd = {m: v for m, v in cos_of.items() if m % 2}
    sin_odd = {m: v for m, v in sin_of.items() if m % 2}
    for n in range(half // 2 + 1):
        c = weighted([(math.cos(angle(n, m, period)), v) for m, v in cos_odd.items()])
        s = weighted([(math.sin(angle(n, m, period)), v) for m, v in sin_odd.items()])
        odd[n] = add(c, s)
        if n and half - n != n:
            odd[half - n] = sub(s, c)
    cos_even = {m // 2: v for m, v in cos_of.items() if m % 2 == 0}
    sin_even = {m // 2: v for m, v in sin_of.items() if m % 2 == 0}
    if not cos_even:
        return [odd[n] for n in range(half)] + [sub(None, odd[n]) for n in range(half)]
    even = synth(cos_even, sin_even, half)
    return [add(even[n], odd[n]) for n in range(half)] + [sub(even[n], odd[n]) for n in range(half)]


def analyse(x, orders, period):
    if period % 2:
        plus = {n: (x[n] + x[period - n] if n else x[0]) for n in range((period + 1) // 2)}
        minus = {n: x[n] - x[period - n] for n in range(1, (period + 1) // 2)}
        cos_of = {m: weighted([(math.cos(angle(n, m, period)), v) for n, v in plus.items()]) for m in orders}
        sin_of = {m: weighted([(math.sin(angle(n, m, period)), v) for n, v in minus.items()]) for m in orders}
        return cos_of, sin_of
    half = period // 2
    odd = [x[n] - x[n + half] for n in range(half)]
    cos_in, sin_in = {}, {}
    for n in range(half // 2 + 1):
        if n and half - n != n:
            cos_in[n] = odd[n] - odd[half - n]
            sin_in[n] = odd[n] + odd[half - n]
        else:
            cos_in[n] = odd[n]
            sin_in[n] = odd[n]
    cos_of = {m: weighted([(math.cos(angle(n, m, period)), v) for n, v in cos_in.items()]) for m in orders if m % 2}
    sin_of = {m: weighted([(math.sin(angle(n, m, period)), v) for n, v in sin_in.items()]) for m in orders if m % 2}
    lower = [m // 2 for m in orders if m % 2 == 0]
    if lower:
        even = [x[n] + x[n + half] for n in range(half)]
        cos_even, sin_even = analyse(even, lower, half)
        cos_of.update({2 * m: v for m, v in cos_even.items()})
        sin_of.update({2 * m: v for m, v in sin_even.items()})
    return cos_of, sin_of


def lane_sum(rows, upward):
    width = rows.shape[1]
    source = lax.broadcasted_iota(jnp.int32, (2 * width, width), 0)
    source = jnp.where(source >= width, source - width, source)
    target = lax.broadcasted_iota(jnp.int32, (2 * width, width), 1)
    chosen = source >= target if upward else source <= target
    ones = jnp.where(chosen, 1.0, 0.0).astype(jnp.bfloat16)
    high = rows.astype(jnp.bfloat16)
    low = (rows - high.astype(jnp.float32)).astype(jnp.bfloat16)
    return jnp.dot(jnp.concatenate([high, low], axis=1), ones, preferred_element_type=jnp.float32)


def partner(me, r, groups):
    if groups & (groups - 1) == 0:
        return jnp.bitwise_xor(me, r)
    return lax.rem(me + r, groups)


def origin(me, r, groups):
    if groups & (groups - 1) == 0:
        return jnp.bitwise_xor(me, r)
    return lax.rem(me + groups - r, groups)


def exchange(messages, only_cross=False):
    groups = len(messages)
    taken = [messages[0]] + [None] * (groups - 1)
    for r in list(range(2, groups)) + ([] if only_cross else [1]):
        if groups & (groups - 1) == 0:
            pairs = [(i, i ^ r) for i in range(groups)]
        else:
            pairs = [(i, (i + r) % groups) for i in range(groups)]
        taken[r] = lax.ppermute(messages[r], "sample", pairs)
    return taken


def tiles_for(rows, quarter):
    return -(-rows // quarter)


VMEM = pl.BlockSpec(memory_space=pltpu.VMEM)
SMEM = pl.BlockSpec(memory_space=pltpu.SMEM)
HBM = pl.BlockSpec(memory_space=pltpu.HBM)
ANY = pl.BlockSpec(memory_space=pl.ANY)
LITTLE = pl.CostEstimate(flops=1000, bytes_accessed=1000, transcendentals=0)


class Chunk:
    def __init__(self, kind, lo, hi, at=0):
        self.at = at
        self.kind, self.lo, self.hi, self.n = kind, lo, hi, hi - lo
        self.q_from = 1 if kind == 1 else 0
        self.q_to = self.n if kind == 2 else self.n + 1
        self.nq = self.q_to - self.q_from
        self.h_from = 1 if kind == 0 else 0
        self.h_to = self.n + 1 if kind == 2 else self.n
        self.nh = self.h_to - self.h_from + (1 if kind == 1 else 0)

    def sent(self, coefs, quarter):
        return 2 * coefs * (self.n + self.nq) + tiles_for(2 * coefs * self.n, quarter)

    def back(self, coefs, quarter):
        return coefs * (self.nh + self.n) + tiles_for(coefs * self.n, quarter)


def gauge_kernel(chunks, groups, has_halo, me_ref, state_ref, adjoint_ref, *rest):
    if has_halo:
        halo_ref, rest = rest[0], rest[1:]
    outs = [rest[:groups]]
    rest = rest[groups:]
    for _ in chunks[1:]:
        outs.append((*outs[0][:2], *rest[: groups - 2]))
        rest = rest[groups - 2 :]
    if not has_halo:
        first_ref, first_sems = rest[0], rest[-1]
        rest = rest[1:-1]
    coefs, parts, planes, rows, width = state_ref.shape
    quarter = rows // groups
    me = me_ref[0]
    sources = (state_ref, adjoint_ref)
    copies = {}
    for which in range(2):
        for at, chunk in enumerate(chunks):
            held, sems = rest[5 * at], rest[5 * at + 4]
            planes_here = pl.ds(chunk.lo, held.shape[3])
            for c in range(coefs):
                copy = pltpu.make_async_copy(sources[which].at[c, :, planes_here], held.at[which, c], sems.at[which, c])
                copy.start()
                copies[which, at, c] = copy
    firsts = []
    if not has_halo:
        for which in range(2):
            for c in range(coefs):
                source = sources[which].at[c, pl.ds(1, 2), 0]
                firsts.append(pltpu.make_async_copy(source, first_ref.at[which, c], first_sems.at[which, c]))
                firsts[-1].start()
    for which in range(2):
        for at, chunk in enumerate(chunks):
            held, phi_held, p_held, q_held, _ = rest[5 * at : 5 * at + 5]
            n, nq = chunk.n, chunk.nq
            own = held.shape[3]
            last_row = lax.broadcasted_iota(jnp.int32, (n + 1, rows, width), 1) == rows - 1
            zero_rows = jnp.zeros((n, quarter, width), jnp.float32)
            for c in range(coefs):
                copies[which, at, c].wait()
            third = held[which, :, 2]
            if own == n:
                third = jnp.concatenate([third, halo_ref[which, :, 1][:, None]], axis=1)
            phi_all = lane_sum(third.reshape(coefs * (n + 1) * rows, width), True)
            phi_held[...] = phi_all.reshape(coefs, n + 1, rows, width)
            for c in range(coefs):
                second = held[which, c, 1]
                if own == n:
                    second = jnp.concatenate([second, halo_ref[which, c, 0][None]], axis=0)
                phi = phi_held[c]
                phi_up = jnp.where(last_row, 0.0, pltpu.roll(phi, rows - 1, 1))
                p_held[which, c, :, 0:rows] = held[which, c, 0, 0:n] + phi[1:] - phi[:-1]
                p_held[which, c, :, rows : rows + quarter] = zero_rows
                q_held[which, c] = (second + (phi_up - phi))[chunk.q_from : chunk.q_to]
            for c in range(coefs):
                for r in range(groups):
                    out_ref = outs[at][r]
                    top = chunk.at if r < 2 else 0
                    base = top + (which * coefs + c) * (n + nq)
                    start = pl.multiple_of(partner(me, r, groups) * quarter, quarter)
                    out_ref[base : base + n] = p_held[which, c, :, pl.ds(start, quarter)]
                    out_ref[base + n : base + n + nq] = q_held[which, c, :, pl.ds(start, quarter)]
                    for i in range(n):
                        spot = (which * coefs + c) * n + i
                        edge = p_held[which, c, i, pl.ds(pl.multiple_of(start + quarter, quarter), quarter)]
                        tile = top + 2 * coefs * (n + nq) + spot // quarter
                        out_ref[tile, spot % quarter : spot % quarter + 1] = edge[0:1]
    for copy in firsts:
        copy.wait()


def gauge(chunks, groups, me, state_hat, adjoint_hat, halo=None):
    coefs, parts, planes, rows, width = state_hat.shape
    quarter = rows // groups
    tiles = [chunk.sent(coefs, quarter) for chunk in chunks]
    counts = [sum(tiles)] * 2 + [t for t in tiles for _ in range(groups - 2)]
    shapes = [jax.ShapeDtypeStruct((t, quarter, width), jnp.float32) for t in counts]
    scratch = []
    for chunk in chunks:
        own = min(chunk.n + 1, planes - chunk.lo)
        scratch += [
            pltpu.VMEM((2, coefs, parts, own, rows, width), jnp.float32),
            pltpu.VMEM((coefs, chunk.n + 1, rows, width), jnp.float32),
            pltpu.VMEM((2, coefs, chunk.n, rows + quarter, width), jnp.float32),
            pltpu.VMEM((2, coefs, chunk.nq, rows, width), jnp.float32),
            pltpu.SemaphoreType.DMA((2, coefs)),
        ]
    operands, specs = [me, state_hat, adjoint_hat], [SMEM, HBM, HBM]
    if halo is None:
        shapes.append(jax.ShapeDtypeStruct((2, coefs, 2, rows, width), jnp.float32))
        scratch.append(pltpu.SemaphoreType.DMA((2, coefs)))
    else:
        operands.append(halo)
        specs.append(VMEM)
    return pl.pallas_call(
        functools.partial(gauge_kernel, chunks, groups, halo is not None),
        in_specs=specs,
        out_specs=[VMEM] * len(shapes),
        out_shape=shapes,
        scratch_shapes=scratch,
        compiler_params=pltpu.CompilerParams(vmem_limit_bytes=FIRST_LIMIT if halo is None else GAUGE_LIMIT),
        cost_estimate=LITTLE,
        name="gauge_middle" if halo is None else "gauge_ends",
    )(*operands)


def sample_kernel(chunk, groups, coefs, later, *refs):
    n, nq, kind = chunk.n, chunk.nq, chunk.kind
    me_ref, message_refs, refs = refs[0], refs[1 : 1 + groups], refs[1 + groups :]
    density_ref, region_ref, refs = refs[0], refs[1], refs[2:]
    edge_q_ref = edge_h_ref = None
    if kind:
        edge_q_ref, edge_h_ref, refs = refs[0], refs[1], refs[2:]
    carried_refs = ()
    if kind == 2:
        carried_refs, refs = refs[: groups - 1], refs[groups - 1 :]
    refs = refs[later:]
    out_refs, grad_ref, refs = refs[:groups], refs[groups], refs[groups + 1 :]
    if kind == 0:
        first_q_ref, last_q_ref, pending_ref, last_psi_ref = refs[:4]
        refs = refs[4:]
    p_ref, q_ref, edge_ref, time_ref, third_ref, psi_ref, h0_ref, h1_ref, tail_ref = refs
    quarter, width = p_ref.shape[4:]
    shape = (quarter, width)
    me = me_ref[0]
    row = lax.broadcasted_iota(jnp.int32, shape, 0)
    lane = lax.broadcasted_iota(jnp.int32, shape, 1)
    last_lane = lane == width - 1
    last_row = row == quarter - 1
    first_row = row == 0
    my_rows = pl.ds(pl.multiple_of(me * quarter, quarter), quarter)
    total_coefs = groups * coefs
    orders = list(range(1, total_coefs // 2 + 1))
    place = [(c // coefs, c % coefs) for c in range(total_coefs)]

    for r in range(groups):
        g = origin(me, r, groups)
        top = chunk.at if r < 2 else 0
        for which in range(2):
            for c in range(coefs):
                base = top + (which * coefs + c) * (n + nq)
                p_ref[which, g, c] = message_refs[r][base : base + n]
                q_ref[which, g, c, chunk.q_from : chunk.q_to] = message_refs[r][base + n : base + n + nq]
        for t in range(tiles_for(2 * coefs * n, quarter)):
            edge_ref[g, t * quarter : (t + 1) * quarter] = message_refs[r][top + 2 * coefs * (n + nq) + t]
    for which in range(2):
        for g in range(groups):
            for c in range(coefs):
                if kind == 0:
                    first_q_ref[which, g, c] = q_ref[which, g, c, 0]
                    last_q_ref[which, g, c] = q_ref[which, g, c, n]
                elif kind == 1:
                    q_ref[which, g, c, 0] = edge_q_ref[which, g, c]
                else:
                    q_ref[which, g, c, n] = edge_q_ref[which, g, c]
    if kind == 1:
        psi_ref[...] = edge_h_ref[...]
    else:
        psi_ref[...] = jnp.zeros(psi_ref.shape, jnp.float32)

    def next_lane(v):
        return jnp.where(last_lane, 0.0, pltpu.roll(v, width - 1, 1))

    def one_plane(i, carry):
        for which in range(2):
            for part in range(3):
                flux = []
                for g, c in place:
                    if part == 0:
                        q = q_ref[which, g, c, i]
                        flux.append(q - next_lane(q))
                    elif part == 1:
                        p = p_ref[which, g, c, i]
                        flux.append(next_lane(p) - p)
                    else:
                        p = p_ref[which, g, c, i]
                        edge = edge_ref[g, pl.ds((which * coefs + c) * n + i, 1), :]
                        up = jnp.where(last_row, jnp.broadcast_to(edge, shape), pltpu.roll(p, quarter - 1, 0))
                        flux.append(q_ref[which, g, c, i + 1] - q_ref[which, g, c, i] - (up - p))
                samples = synth({m: flux[2 * m - 2] for m in orders}, {m: flux[2 * m - 1] for m in orders}, NT)
                for k in range(NT):
                    time_ref[which * 3 + part, k] = samples[k]
        density = density_ref[chunk.lo + i, my_rows]
        region = region_ref[chunk.lo + i, my_rows]
        iron = region == 0
        share = jnp.where(iron, density * density * density, 0.0) * (1.0 - iron_floor)
        slope = jnp.where(iron, 3.0 * density * density, 0.0)
        base = jnp.where(region == 1, magnet_reluct, 1.0)
        total = jnp.zeros(shape, jnp.float32)
        for k in range(NT):
            b = [time_ref[j, k] for j in range(3)]
            a = [time_ref[3 + j, k] for j in range(3)]
            square = b[0] * b[0] + b[1] * b[1] + b[2] * b[2]
            inner = b[0] * a[0] + b[1] * a[1] + b[2] * a[2]
            inverse = 1.0 / (square + saturation)
            scaled = share * inverse
            reluct_now = base - scaled
            ratio = inverse * inner
            total = total + ratio
            along = scaled * ratio
            along = along + along
            for j in range(3):
                time_ref[j, k] = reluct_now * a[j] + along * b[j]
        grad_ref[i] = ((1.0 - iron_floor) / NT) * slope * total
        for part in (2, 0, 1):
            cos_of, sin_of = analyse([time_ref[part, k] for k in range(NT)], orders, NT)
            field = []
            for m in orders:
                field += [cos_of[m], sin_of[m]]
            if part == 2:
                for at in range(total_coefs):
                    third_ref[at] = field[at]
                psi = lane_sum(third_ref[...].reshape(total_coefs * quarter, width), False)
                third_ref[...] = psi.reshape(total_coefs, quarter, width)
            elif part == 0:
                for at, (g, c) in enumerate(place):
                    h0_ref[g, c, i] = field[at] + (psi_ref[g, c] - third_ref[at])
            else:
                for at, (g, c) in enumerate(place):
                    psi = third_ref[at]
                    down = jnp.where(first_row, 0.0, pltpu.roll(psi, 1, 0))
                    h1_ref[g, c, i] = field[at] + (down - psi)
                    tail_ref[g, pl.ds(c * n + i, 1), :] = psi[quarter - 1 : quarter]
                    psi_ref[g, c] = psi
        return carry

    lax.fori_loop(0, n, one_plane, 0)
    for g, c in place:
        if kind == 0:
            pending_ref[g, c] = h0_ref[g, c, 0]
            last_psi_ref[g, c] = psi_ref[g, c]
        elif kind == 1:
            h0_ref[g, c, n] = psi_ref[g, c]
        else:
            h0_ref[g, c, n] = edge_h_ref[g, c] + psi_ref[g, c]
    step = chunk.nh + n
    for r in range(groups):
        g = partner(me, r, groups)
        for c in range(coefs):
            out_refs[r][c * step : c * step + chunk.nh] = h0_ref[g, c, chunk.h_from : chunk.h_from + chunk.nh]
            out_refs[r][c * step + chunk.nh : (c + 1) * step] = h1_ref[g, c]
        for t in range(tiles_for(coefs * n, quarter)):
            out_refs[r][coefs * step + t] = tail_ref[g, t * quarter : (t + 1) * quarter]
    for r, carried_ref in enumerate(carried_refs, 1):
        out_refs[r][chunk.back(coefs, quarter) :] = carried_ref[...]


def sample_fields(chunk, me, messages, density, region, coefs, edges, after):
    groups = len(messages)
    _, quarter, width = messages[0].shape
    n = chunk.n
    f32 = jnp.float32
    shapes = [jax.ShapeDtypeStruct((chunk.back(coefs, quarter), quarter, width), f32)] * groups
    if chunk.kind == 2:
        both = chunk.back(coefs, quarter) + edges[2].shape[0]
        shapes[1:] = [jax.ShapeDtypeStruct((both, quarter, width), f32)] * (groups - 1)
    shapes.append(jax.ShapeDtypeStruct((n, quarter, width), f32))
    if chunk.kind == 0:
        shapes += [jax.ShapeDtypeStruct((2, groups, coefs, quarter, width), f32)] * 2
        shapes += [jax.ShapeDtypeStruct((groups, coefs, quarter, width), f32)] * 2
    operands = [me, *messages, density, region, *edges, *after]
    return pl.pallas_call(
        functools.partial(sample_kernel, chunk, groups, coefs, len(after)),
        in_specs=[SMEM] + [VMEM] * (len(operands) - 1 - len(after)) + [ANY] * len(after),
        out_specs=[VMEM] * len(shapes),
        out_shape=shapes,
        scratch_shapes=[
            pltpu.VMEM((2, groups, coefs, n, quarter, width), f32),
            pltpu.VMEM((2, groups, coefs, n + 1, quarter, width), f32),
            pltpu.VMEM((groups, tiles_for(2 * coefs * n, quarter) * quarter, width), f32),
            pltpu.VMEM((6, NT, quarter, width), f32),
            pltpu.VMEM((groups * coefs, quarter, width), f32),
            pltpu.VMEM((groups, coefs, quarter, width), f32),
            pltpu.VMEM((groups, coefs, n + 1, quarter, width), f32),
            pltpu.VMEM((groups, coefs, n, quarter, width), f32),
            pltpu.VMEM((groups, tiles_for(coefs * n, quarter) * quarter, width), f32),
        ],
        compiler_params=pltpu.CompilerParams(vmem_limit_bytes=SAMPLE_LIMIT),
        cost_estimate=LITTLE,
        name="samples%d" % chunk.kind,
    )(*operands)


def last_plane_kernel(chunk, coefs, me_ref, *refs):
    groups = len(refs) - 3
    message_refs, out_ref, row_ref = refs[:groups], refs[groups + 1], refs[groups + 2]
    quarter, width = message_refs[0].shape[1:]
    rows = quarter * groups
    step = chunk.nh + chunk.n
    me = me_ref[0]
    for c in range(coefs):
        for r in range(groups):
            here = pl.ds(pl.multiple_of(origin(me, r, groups) * quarter, quarter), quarter)
            row_ref[c, here] = message_refs[r][(c + 1) * step - 1]
            out_ref[c, 1, here] = message_refs[r][c * step + chunk.nh - 1]
        for r in range(groups):
            add_edge(row_ref.at[c], message_refs[r], chunk, coefs, c * chunk.n + chunk.n - 1, origin(me, r, groups) * quarter + quarter)
        out_ref[c, 0] = row_ref[c, 0:rows]


def add_edge(target, message_ref, chunk, coefs, spot, row, shift=0):
    quarter = message_ref.shape[1]
    tile = shift + coefs * (chunk.nh + chunk.n) + spot // quarter
    here = pl.ds(pl.multiple_of(row, quarter), 1)
    target[here] = target[here] + message_ref[tile, spot % quarter : spot % quarter + 1]


def last_plane(chunk, me, messages, coefs, after):
    groups = len(messages)
    _, quarter, width = messages[0].shape
    rows = groups * quarter
    return pl.pallas_call(
        functools.partial(last_plane_kernel, chunk, coefs),
        in_specs=[SMEM] + [VMEM] * groups + [ANY],
        out_specs=VMEM,
        out_shape=jax.ShapeDtypeStruct((coefs, 2, rows, width), jnp.float32),
        scratch_shapes=[pltpu.VMEM((coefs, rows + quarter, width), jnp.float32)],
        compiler_params=pltpu.CompilerParams(vmem_limit_bytes=LAST_LIMIT),
        cost_estimate=LITTLE,
        name="last_plane",
    )(me, *messages, after)


def residual_kernel(chunks, shifts, groups, coefs, me_ref, *refs):
    message_refs = [refs[k * groups : (k + 1) * groups] for k in range(len(chunks))]
    refs = refs[len(chunks) * groups :]
    halo_ref, objective_ref, out_ref, h0_ref, h1_ref, given, give_sems = refs
    parts, planes, rows, width = objective_ref.shape[1:]
    quarter = rows // groups
    me = me_ref[0]
    row = lax.broadcasted_iota(jnp.int32, (rows, width), 0)
    lane = lax.broadcasted_iota(jnp.int32, (rows, width), 1)
    gives = [pltpu.make_async_copy(given.at[c], out_ref.at[c], give_sems.at[c]) for c in range(coefs)]

    def lower_lane(v):
        return jnp.where(lane == 0, 0.0, pltpu.roll(v, 1, 1))

    for c in range(coefs):
        for chunk, shift, messages in zip(chunks, shifts, message_refs):
            step = chunk.nh + chunk.n
            from_h0, to_h0 = chunk.lo + chunk.h_from, chunk.lo + chunk.h_to
            for r in range(groups):
                here = pl.ds(pl.multiple_of(origin(me, r, groups) * quarter, quarter), quarter)
                at = shift[r] + c * step
                h0_ref[c, from_h0:to_h0, here] = messages[r][at : at + to_h0 - from_h0]
                h1_ref[c, chunk.lo : chunk.hi, here] = messages[r][at + chunk.nh : at + step]
            for r in range(groups):
                above = origin(me, r, groups) * quarter + quarter
                for i in range(chunk.n):
                    add_edge(h1_ref.at[c, chunk.lo + i], messages[r], chunk, coefs, c * chunk.n + i, above, shift[r])
        before = halo_ref[c, 0]
        for i in range(planes):
            h0 = h0_ref[c, i]
            if i == 0:
                h0 = h0 + halo_ref[c, 1]
            h1 = h1_ref[c, i, 0:rows]
            given[c, 0, i] = objective_ref[c, 0, i] - (2.0 / NT) * (lower_lane(h1) - h1)
            given[c, 1, i] = objective_ref[c, 1, i] - (2.0 / NT) * (h0 - lower_lane(h0))
            lower_row = jnp.where(row == 0, 0.0, pltpu.roll(h0, 1, 0))
            given[c, 2, i] = objective_ref[c, 2, i] - (2.0 / NT) * ((lower_row - h0) - (before - h1))
            before = h1
        gives[c].start()
    for copy in gives:
        copy.wait()


def residual(chunks, shifts, me, returned, objective_hat, halo):
    coefs, parts, planes, rows, width = objective_hat.shape
    groups = len(returned[0])
    quarter = rows // groups
    operands = [me] + [m for messages in returned for m in messages] + [halo, objective_hat]
    return pl.pallas_call(
        functools.partial(residual_kernel, chunks, shifts, groups, coefs),
        in_specs=[SMEM] + [VMEM] * (len(operands) - 1),
        out_specs=HBM,
        out_shape=jax.ShapeDtypeStruct(objective_hat.shape, jnp.float32),
        scratch_shapes=[
            pltpu.VMEM((coefs, planes, rows, width), jnp.float32),
            pltpu.VMEM((coefs, planes, rows + quarter, width), jnp.float32),
            pltpu.VMEM((coefs, parts, planes, rows, width), jnp.float32),
            pltpu.SemaphoreType.DMA((coefs,)),
        ],
        compiler_params=pltpu.CompilerParams(vmem_limit_bytes=RESIDUAL_LIMIT),
        cost_estimate=LITTLE,
        name="residual",
    )(*operands)


def local(state_hat, adjoint_hat, objective_hat, density, region):
    groups = lax.axis_size("sample")
    coefs, parts, planes, rows, width = state_hat.shape
    me = lax.axis_index("sample").astype(jnp.int32).reshape(1)
    first = planes // 4
    last = planes - first
    middle_chunk, last_chunk = Chunk(0, first, last), Chunk(1, last, planes)
    first_chunk = Chunk(2, 0, first, last_chunk.sent(coefs, rows // groups))
    *sent0, first_planes = gauge((middle_chunk,), groups, me, state_hat, adjoint_hat)
    cells0 = exchange(sent0)
    upper = passed_along(first_planes, "space", -1)
    sent1 = gauge((last_chunk, first_chunk), groups, me, state_hat, adjoint_hat, upper)
    cells1 = exchange(sent1[:groups])
    cells2 = cells1[:2] + exchange([None, None, *sent1[groups:]], only_cross=True)[2:]
    *out0, grad0, first_q, last_q, pending, last_psi = sample_fields(middle_chunk, me, cells0, density, region, coefs, (), sent1[:1])
    *out1, grad1 = sample_fields(last_chunk, me, cells1, density, region, coefs, (last_q, last_psi), ())
    back1 = exchange(out1)
    *out2, grad2 = sample_fields(first_chunk, me, cells2, density, region, coefs, (first_q, pending, *out0[1:]), out1[:1])
    back2 = exchange(out2)
    back0 = [out0[0], *back2[1:]]
    none = [0] * groups
    carried = [0] + [first_chunk.back(coefs, rows // groups)] * (groups - 1)
    lower = passed_along(last_plane(last_chunk, me, back1, coefs, out2[0]), "space", 1)
    chunks = (middle_chunk, last_chunk, first_chunk)
    adjoint_residual = residual(chunks, (carried, none, none), me, (back0, back1, back2), objective_hat, lower)
    return adjoint_residual, jnp.concatenate([grad2, grad0, grad1], axis=0)


def solution(mesh):
    in_specs = (
        P("sample", None, "space", None, None),
        P("sample", None, "space", None, None),
        P("sample", None, "space", None, None),
        P("space", None, None),
        P("space", None, None),
    )
    out_specs = (P("sample", None, "space", None, None), P("space", "sample", None))
    return jax.shard_map(local, mesh=mesh, in_specs=in_specs, out_specs=out_specs, check_vma=False)
```
